256 devices in a mesh: rows: 32 (over x, y, core), feat: 8 (over z).
Axes of the slice: x: 4, y: 4, z: 8, core: 2. Of those that a mesh axis runs over, the one named last changes fastest.
Arguments:
- fact_table: bfloat16 [65536, 1024], P('rows', 'feat'), may hold values from -6 to 6
- dim_table: bfloat16 [131072, 1024], P('rows', 'feat'), may hold values from -6 to 6
- fact_weight: float32 [1024], P('feat'), may hold values from -0.125 to 0.125
- dim_weight: float32 [1024], P('feat'), may hold values from -0.125 to 0.125
- bucket: int32 [65536, 1], P('rows'), may hold values from 0 to 31; in each aligned block of 2048 rows (0 to 2047, 2048 to 4095, ...) at most 128 rows name the same one
- row_index: int32 [65536], P('rows'), may hold values from 0 to 4095
- labels: int32 [65536], P('rows'), may hold values 0 or 1
Outputs:
- new_fact_weight: float32 [1024], P('feat')
- new_dim_weight: float32 [1024], P('feat')
- fact_prob: float32 [65536], P('rows')
The draws below stay inside these ranges and needn't reach their ends.
Inputs may be any that keep to these rules, and one draw needn't show every extreme that they name: `bucket`: among the rows of one device no owner is named by more than 128 rows, a bound that some block reaches.
All inputs are finite; a program needn't handle non-finite values. No bound on the sum of `labels` on one device may be relied on, other than what follows from the above.
Results may differ from the reference program's by a relative error of at most 0.0003.
Values may be sent and summed in bfloat16 or wider, within the bound.
No kernel may reach another device: no remote copies, remote signals or barrier semaphores. Data moves between devices by JAX's collectives and lax.ppermute only.
A program may use at most 64 MiB of HBM per device.

```python
import math
import jax
import jax.numpy as jnp
import numpy as np
from jax import lax

FD = 1024
DA = 1024
FACT_DEV = 2048
DIM_DEV = 4096
CAP = 128
FACTS = 65536
DIMROWS = 131072
N_ROWS = 32


def with_ends(result, rng, low, high):
    longest = result.shape.index(max(result.shape))
    spots = []
    for shift in (0, 1):
        where = [jax.random.randint(jax.random.fold_in(rng, axis), (), 0, length) for axis, length in enumerate(result.shape)]
        where[longest] = (where[longest] + shift) % result.shape[longest]
        spots.append(tuple(where))
    return result.at[spots[0]].set(low).at[spots[1]].set(high)


def block_levels(key, extent, shards, smallest, high):
    def one(position, blocks):
        steps = jax.random.uniform(jax.random.fold_in(jax.random.fold_in(key, 6), position), (blocks,), jnp.float32, smallest / len(shards), high / len(shards))
        return jnp.repeat(jnp.exp(steps), extent[position] // blocks).reshape((-1,) + (1,) * (len(extent) - position - 1))

    factor_of = one(*shards[0])
    for cut in shards[1:]:
        factor_of = factor_of * one(*cut)
    return factor_of


def routed_block(rng, own, number, rows, amount, top, bound, slope):
    sequence = jax.random.permutation(rng, amount)
    heavy_load, ordinary = shares(amount, rows * top, bound, slope, True), shares(amount, rows * top, bound, slope, False)
    places = jnp.arange(amount)

    def named(lengths, rotation):
        used = int((lengths > 0).sum())
        fixed = max(1, used // 4)
        moved = fixed + (places - fixed + rotation * (used - fixed)) % max(1, amount - fixed)
        return jnp.zeros((amount,), jnp.int32).at[sequence[jnp.where(places < fixed, places, moved)]].set(jnp.asarray(lengths, jnp.int32))

    lengths = jnp.where(number % 4 == 0, named(heavy_load, number // 4), named(ordinary, number - number // 4 - 1))
    mixed = jax.random.permutation(jax.random.fold_in(own, 3), amount)
    source_of, receiver = mixed[0:amount // 2 * 2:2], mixed[1:amount // 2 * 2:2]
    margin = jnp.minimum(lengths[source_of] - 1, bound - lengths[receiver]) // 2
    margin = jnp.where((source_of == sequence[0]) | (receiver == sequence[0]) | (lengths[receiver] == 0), 0, jnp.maximum(margin, 0))
    moved = jax.random.randint(jax.random.fold_in(own, 4), (amount // 2,), 0, 1 << 20) % (margin + 1)
    lengths = lengths.at[source_of].add(-moved).at[receiver].add(moved)
    items = jnp.searchsorted(jnp.cumsum(lengths), jnp.arange(rows * top), side="right").astype(jnp.int32)
    table = items.reshape(top, rows).T
    table = table[jax.random.permutation(jax.random.fold_in(own, 1), rows)]
    rotation = jax.random.randint(jax.random.fold_in(own, 2), (rows, 1), 0, top)
    return jnp.take_along_axis(table, (jnp.arange(top)[None, :] + rotation) % top, axis=1)


def shares(number_of, total, reach, lean, full):
    weights = [(1 << 20) // math.isqrt(standing ** lean) + 1 for standing in range(1, number_of + 1)]
    largest = reach if full else min(reach, max(-(-total // number_of), total * weights[0] // sum(weights)))
    least = 1 if total - largest >= number_of - 1 else 0
    holding, surplus = [largest] + [least] * (number_of - 1), total - largest - least * (number_of - 1)
    while surplus > 0:
        movable = [i for i in range(1, number_of) if holding[i] < largest] or [i for i in range(1, number_of) if holding[i] < reach]
        whole, budget = sum([weights[i] for i in movable]), surplus
        for i in movable:
            addition = min(reach - holding[i], max(1, budget * weights[i] // whole), surplus)
            holding[i] = holding[i] + addition
            surplus = surplus - addition
    return np.array(holding)


def centred(own_key, extent, deviation, bound, shards=(), held_as=jnp.bfloat16):
    values = deviation * jax.random.normal(own_key, extent, jnp.float32)
    if shards:
        values = values * block_levels(own_key, extent, shards, -0.22, 0.18)
    return jnp.clip(values, -bound, bound).astype(held_as)


def setup_inputs(seed: int = 0) -> dict:
    streams_of = jax.random.split(jax.random.key(seed), 8)
    fact_table = centred(streams_of[0], (FACTS, FD), 1.0, 6.0, ((0, 32), (1, 8)))
    dim_table = centred(streams_of[1], (DIMROWS, DA), 1.0, 6.0, ((0, 32), (1, 8)))
    fact_weight = centred(streams_of[2], (FD,), (FD + DA) ** -0.5, 0.125, ((0, 8),), jnp.float32)
    dim_weight = centred(streams_of[3], (DA,), (FD + DA) ** -0.5, 0.125, ((0, 8),), jnp.float32)
    bucket_keys = jax.random.split(jax.random.fold_in(streams_of[4], 1), FACTS // FACT_DEV)
    bucket_turns = jax.random.permutation(jax.random.fold_in(streams_of[4], 3), FACTS // FACT_DEV)
    bucket = jax.vmap(lambda own, number: routed_block(jax.random.fold_in(streams_of[4], 2), own, number, FACT_DEV, N_ROWS, 1, CAP, 2))(bucket_keys, bucket_turns).reshape((FACTS, 1))
    row_index = with_ends(jax.random.randint(streams_of[5], (FACTS,), 0, DIM_DEV), jax.random.fold_in(streams_of[5], 1), 0, DIM_DEV - 1).astype(jnp.int32)
    labels = with_ends((jax.random.randint(streams_of[6], (FACTS,), 0, 2) < 1).astype(jnp.int32), jax.random.fold_in(streams_of[6], 1), 0, 1)
    return dict(fact_table=fact_table, dim_table=dim_table, fact_weight=fact_weight, dim_weight=dim_weight, bucket=bucket, row_index=row_index, labels=labels)


def reference(fact_table, dim_table, fact_weight, dim_weight, bucket, row_index, labels):
    joined_row = (bucket[:, 0] * DIM_DEV + row_index).astype(jnp.int32)
    dim_score = jnp.dot(dim_table.astype(jnp.float32), dim_weight, precision=lax.Precision.HIGHEST)
    logits = jnp.dot(fact_table.astype(jnp.float32), fact_weight, precision=lax.Precision.HIGHEST) + dim_score[joined_row]
    fact_prob = jax.nn.sigmoid(logits)
    residual = fact_prob - labels.astype(jnp.float32)
    grad_scale = 1.0 / jnp.sqrt(jnp.float32(FACTS))
    grad_fact = jnp.dot(residual, fact_table.astype(jnp.float32), precision=lax.Precision.HIGHEST) * grad_scale
    per_row = jax.ops.segment_sum(residual, joined_row, num_segments=DIMROWS)
    grad_dim = jnp.dot(per_row, dim_table.astype(jnp.float32), precision=lax.Precision.HIGHEST) * grad_scale
    return (fact_weight - 0.5 * grad_fact, dim_weight - 0.5 * grad_dim, fact_prob)
```

```python
import jax
import jax.numpy as jnp
from jax import lax
from jax.experimental import pallas as pl
from jax.experimental.pallas import tpu as pltpu
from jax.sharding import PartitionSpec as P

LANES = 128
OWNERS = 32
PEERS = 8
DIM_ROWS = 32
FACT_ROWS = 16
FACTS_HERE = FACT_ROWS * LANES
SCORE_ROWS = DIM_ROWS + FACT_ROWS
BLOCK_ROWS = DIM_ROWS + 2
LABEL_BIT = 12
VALID_BIT = 13

bf16 = jnp.bfloat16
f32 = jnp.float32


def split3(value):
    high = value.astype(bf16).astype(f32)
    rest = value - high
    middle = rest.astype(bf16).astype(f32)
    return high, middle, rest - middle


def stacked_row(row):
    shape = (8, row.shape[1])
    place = lax.broadcasted_iota(jnp.int32, shape, 0)
    high, middle, low = split3(row)
    return jnp.where(
        place == 0, high, jnp.where(place == 1, middle, jnp.where(place == 2, low, 0.0))
    ).astype(bf16)


def dot_nt(left, right):
    return lax.dot_general(
        left, right, (((1,), (1,)), ((), ())), preferred_element_type=f32
    )


def dot_nn(left, right):
    return jnp.dot(left, right, preferred_element_type=f32)


def hits(row, count):
    return lax.broadcasted_iota(jnp.int32, (count, row.shape[1]), 0) == row


def onehot(row, count):
    return jnp.where(hits(row, count), 1.0, 0.0).astype(bf16)


def scores_kernel(fact_ref, dim_ref, fact_weight_ref, dim_weight_ref, out_ref):
    dim_part = jnp.sum(dot_nt(stacked_row(dim_weight_ref[...]), dim_ref[...]), 0, keepdims=True)
    fact_part = jnp.sum(dot_nt(stacked_row(fact_weight_ref[...]), fact_ref[...]), 0, keepdims=True)
    for i in range(DIM_ROWS):
        out_ref[0, i : i + 1, :] = dim_part[:, i * LANES : (i + 1) * LANES]
    for i in range(FACT_ROWS):
        out_ref[0, DIM_ROWS + i : DIM_ROWS + i + 1, :] = fact_part[:, i * LANES : (i + 1) * LANES]
    for peer in range(1, PEERS):
        out_ref[peer] = out_ref[0]


def slots_kernel(bucket_ref, index_ref, label_ref, rank_ref, meta_ref):
    width = 2 * LANES
    chunks = FACTS_HERE // width
    bucket = bucket_ref[...]
    owner_hits = onehot(bucket, OWNERS)
    stack = jnp.concatenate(
        [owner_hits[:, c * width : (c + 1) * width] for c in range(chunks)], 0
    )
    upto = jnp.where(
        lax.broadcasted_iota(jnp.int32, (width, width), 0)
        <= lax.broadcasted_iota(jnp.int32, (width, width), 1),
        1.0,
        0.0,
    ).astype(bf16)
    prefix = dot_nn(stack, upto)
    before = jnp.zeros((OWNERS, 1), f32)
    for c in range(chunks):
        here = prefix[c * OWNERS : (c + 1) * OWNERS]
        mine = hits(bucket[:, c * width : (c + 1) * width], OWNERS)
        rank_ref[:, c * width : (c + 1) * width] = (
            jnp.sum(jnp.where(mine, here + before, 0.0), 0, keepdims=True).astype(jnp.int32) - 1
        )
        before = before + here[:, width - 1 : width]
    index = index_ref[...]
    low = (index & (LANES - 1)).astype(f32)
    high = ((index >> 7) + (label_ref[...] << (LABEL_BIT - 7)) + (1 << (VALID_BIT - 7))).astype(f32)
    mine = hits(bucket, OWNERS)
    fields = jnp.concatenate([jnp.where(mine, low, 0.0), jnp.where(mine, high, 0.0)], 0)
    packed = dot_nt(fields.astype(bf16), onehot(rank_ref[...], LANES))
    meta_ref[...] = packed[:OWNERS] + packed[OWNERS:] * LANES


def pack_kernel(recv_ref, bucket_ref, rank_ref, meta_ref, out_ref, dims_ref, facts_ref, left_ref):
    total = recv_ref[0]
    for peer in range(1, PEERS):
        total = total + recv_ref[peer]
    dims_ref[...] = total[:DIM_ROWS]
    for i in range(FACT_ROWS):
        cut = slice(i * LANES, (i + 1) * LANES)
        mine = hits(bucket_ref[:, cut], OWNERS)
        for part, value in enumerate(split3(total[DIM_ROWS + i : DIM_ROWS + i + 1])):
            left_ref[part * OWNERS : (part + 1) * OWNERS, cut] = jnp.where(mine, value, 0.0).astype(bf16)
    packed = dot_nt(left_ref[...], onehot(rank_ref[...], LANES))
    packed = packed[:OWNERS] + packed[OWNERS : 2 * OWNERS] + packed[2 * OWNERS :]
    facts_ref[...] = packed
    for owner in range(OWNERS):
        out_ref[owner, :DIM_ROWS, :] = total[:DIM_ROWS]
        out_ref[owner, DIM_ROWS : DIM_ROWS + 1, :] = packed[owner : owner + 1]
        out_ref[owner, DIM_ROWS + 1 : DIM_ROWS + 2, :] = meta_ref[owner : owner + 1, :]


def stacked(value):
    return jnp.concatenate(split3(value), 0).astype(bf16)


def found(parts, row):
    value = parts[:DIM_ROWS] + parts[DIM_ROWS : 2 * DIM_ROWS] + parts[2 * DIM_ROWS :]
    return jnp.sum(jnp.where(hits(row, DIM_ROWS), value, 0.0), 0, keepdims=True)


def sigmoid(value):
    return 1.0 / (1.0 + jnp.exp(-value))


def grads_kernel(
    recv_ref,
    dims_ref,
    facts_ref,
    meta_ref,
    bucket_ref,
    rank_ref,
    label_ref,
    fact_ref,
    dim_ref,
    out_ref,
    prob_ref,
    home_ref,
    own_ref,
    code_ref,
    low_ref,
    left_ref,
):
    meta = meta_ref[...].astype(jnp.int32)
    for owner in range(OWNERS):
        code = meta[owner : owner + 1]
        parts = dot_nn(stacked(recv_ref[owner, :DIM_ROWS, :]), onehot(code & (LANES - 1), LANES))
        home_ref[owner : owner + 1, :] = found(parts, (code >> 7) & (DIM_ROWS - 1))
    dims = stacked(dims_ref[...])
    for source in range(OWNERS):
        cut = slice(source * LANES, (source + 1) * LANES)
        code = recv_ref[source, DIM_ROWS + 1 : DIM_ROWS + 2, :].astype(jnp.int32)
        code_ref[source : source + 1, :] = code
        column = onehot(code & (LANES - 1), LANES)
        low_ref[:, cut] = column
        own_ref[source : source + 1, :] = recv_ref[source, DIM_ROWS : DIM_ROWS + 1, :] + found(
            dot_nn(dims, column), (code >> 7) & (DIM_ROWS - 1)
        )
    prob = sigmoid(home_ref[...] + facts_ref[...])
    parts = dot_nn(stacked(prob), onehot(rank_ref[...], LANES))
    prob = found(parts, bucket_ref[...])
    prob_ref[...] = prob
    residual = prob - label_ref[...].astype(f32)
    grad_fact = jnp.sum(dot_nn(stacked_row(residual), fact_ref[...]), 0, keepdims=True)
    code = code_ref[...]
    residual = (sigmoid(own_ref[...]) - ((code >> LABEL_BIT) & 1).astype(f32)) * (
        code >> VALID_BIT
    ).astype(f32)
    terms = split3(residual)
    for source in range(OWNERS):
        cut = slice(source * LANES, (source + 1) * LANES)
        mine = hits((code[source : source + 1] >> 7) & (DIM_ROWS - 1), DIM_ROWS)
        for part, value in enumerate(terms):
            left_ref[part * DIM_ROWS : (part + 1) * DIM_ROWS, cut] = jnp.where(
                mine, value[source : source + 1], 0.0
            ).astype(bf16)
    sums = dot_nt(left_ref[...], low_ref[...])
    sums = sums[:DIM_ROWS] + sums[DIM_ROWS : 2 * DIM_ROWS] + sums[2 * DIM_ROWS :]
    rows = jnp.concatenate([stacked_row(sums[i : i + 1]) for i in range(DIM_ROWS)], 1)
    grad_dim = jnp.sum(dot_nn(rows, dim_ref[...]), 0, keepdims=True)
    for owner in range(OWNERS):
        out_ref[owner, 0:1, :] = grad_fact
        out_ref[owner, 1:2, :] = grad_dim


def update_kernel(recv_ref, fact_weight_ref, dim_weight_ref, fact_out_ref, dim_out_ref):
    total = recv_ref[0]
    for peer in range(1, OWNERS):
        total = total + recv_ref[peer]
    scale = 0.5 / (OWNERS * FACTS_HERE) ** 0.5
    fact_out_ref[...] = fact_weight_ref[...] - scale * total[0:1]
    dim_out_ref[...] = dim_weight_ref[...] - scale * total[1:2]


def call(kernel, outs, scratch=()):
    return pl.pallas_call(
        kernel,
        out_shape=[jax.ShapeDtypeStruct(shape, dtype) for shape, dtype in outs],
        scratch_shapes=[pltpu.VMEM(shape, dtype) for shape, dtype in scratch],
        compiler_params=pltpu.CompilerParams(vmem_limit_bytes=32 * 1024 * 1024),
    )


def exchange(value, axis):
    return lax.all_to_all(value, axis, split_axis=0, concat_axis=0, tiled=True)


def shards(fact_table, dim_table, fact_weight, dim_weight, bucket, row_index, labels):
    bucket = bucket.reshape(1, FACTS_HERE)
    row_index = row_index.reshape(1, FACTS_HERE)
    labels = labels.reshape(1, FACTS_HERE)
    fact_weight = fact_weight.reshape(1, LANES)
    dim_weight = dim_weight.reshape(1, LANES)

    (partial,) = call(scores_kernel, [((PEERS, SCORE_ROWS, LANES), f32)])(
        fact_table, dim_table, fact_weight, dim_weight
    )
    rank, meta = call(
        slots_kernel, [((1, FACTS_HERE), jnp.int32), ((OWNERS, LANES), f32)]
    )(bucket, row_index, labels)
    partial = exchange(partial, "feat")
    blocks, dims, facts = call(
        pack_kernel,
        [((OWNERS, BLOCK_ROWS, LANES), f32), ((DIM_ROWS, LANES), f32), ((OWNERS, LANES), f32)],
        [((3 * OWNERS, FACTS_HERE), bf16)],
    )(partial, bucket, rank, meta)
    blocks = exchange(blocks, "rows")
    grads, prob = call(
        grads_kernel,
        [((OWNERS, 2, LANES), f32), ((1, FACTS_HERE), f32)],
        [
            ((OWNERS, LANES), f32),
            ((OWNERS, LANES), f32),
            ((OWNERS, LANES), jnp.int32),
            ((LANES, OWNERS * LANES), bf16),
            ((3 * DIM_ROWS, OWNERS * LANES), bf16),
        ],
    )(blocks, dims, facts, meta, bucket, rank, labels, fact_table, dim_table)
    grads = exchange(grads, "rows")
    new_fact, new_dim = call(update_kernel, [((1, LANES), f32), ((1, LANES), f32)])(
        grads, fact_weight, dim_weight
    )
    return new_fact.reshape(-1), new_dim.reshape(-1), prob.reshape(-1)


def solution(mesh):
    return jax.shard_map(
        shards,
        mesh=mesh,
        in_specs=(
            P("rows", "feat"),
            P("rows", "feat"),
            P("feat"),
            P("feat"),
            P("rows", None),
            P("rows"),
            P("rows"),
        ),
        out_specs=(P("feat"), P("feat"), P("rows")),
        check_vma=False,
    )
```

```python
import jax
import jax.numpy as jnp
from jax import lax
from jax.experimental import pallas as pl
from jax.experimental.pallas import tpu as pltpu
from jax.sharding import PartitionSpec as P

LANES = 128
OWNERS = 32
CHIPS = 16
PEERS = 8
DIM_ROWS = 32
FACT_ROWS = 16
FACTS_HERE = FACT_ROWS * LANES
SCORE_ROWS = DIM_ROWS + FACT_ROWS
BLOCK_ROWS = DIM_ROWS + 4
PIECE = 1024
OWNER_BIT = 7
LABEL_BIT = 12
VALID_BIT = 13

bf16 = jnp.bfloat16
f32 = jnp.float32


def split3(value):
    high = value.astype(bf16).astype(f32)
    rest = value - high
    middle = rest.astype(bf16).astype(f32)
    return high, middle, rest - middle


def stacked_row(row):
    shape = (8, row.shape[1])
    place = lax.broadcasted_iota(jnp.int32, shape, 0)
    high, middle, low = split3(row)
    return jnp.where(
        place == 0, high, jnp.where(place == 1, middle, jnp.where(place == 2, low, 0.0))
    ).astype(bf16)


def dot_nt(left, right):
    return lax.dot_general(
        left, right, (((1,), (1,)), ((), ())), preferred_element_type=f32
    )


def dot_nn(left, right):
    return jnp.dot(left, right, preferred_element_type=f32)


def hits(row, count):
    return lax.broadcasted_iota(jnp.int32, (count, row.shape[1]), 0) == row


def onehot(row, count):
    return jnp.where(hits(row, count), 1.0, 0.0).astype(bf16)


def scores_kernel(
    fact_hbm, dim_hbm, fact_weight_hbm, dim_weight_hbm, out_ref, fact, dim, weights, sems
):
    def copies(source, target, first):
        found = []
        for i in range(source.shape[0] // PIECE):
            cut = pl.ds(i * PIECE, PIECE)
            found.append(pltpu.make_async_copy(source.at[cut], target.at[cut], sems.at[first + i]))
        return found

    dim_pieces = copies(dim_hbm, dim, 2)
    fact_pieces = copies(fact_hbm, fact, 2 + len(dim_pieces))
    dim_weight = pltpu.make_async_copy(dim_weight_hbm, weights.at[pl.ds(0, 1)], sems.at[0])
    fact_weight = pltpu.make_async_copy(fact_weight_hbm, weights.at[pl.ds(1, 1)], sems.at[1])
    for copy in [dim_weight, fact_weight] + dim_pieces + fact_pieces:
        copy.start()
    row = 0
    for place, weight, table, pieces in (
        (0, dim_weight, dim, dim_pieces),
        (1, fact_weight, fact, fact_pieces),
    ):
        weight.wait()
        terms = stacked_row(weights[place : place + 1, :])
        for i, piece in enumerate(pieces):
            piece.wait()
            part = dot_nt(terms, table[i * PIECE : (i + 1) * PIECE, :])
            part = jnp.sum(part, 0, keepdims=True)
            for j in range(PIECE // LANES):
                out_ref[0, row : row + 1, :] = part[:, j * LANES : (j + 1) * LANES]
                row += 1
    for peer in range(1, PEERS):
        out_ref[peer] = out_ref[0]


def slots_kernel(core_ref, bucket_hbm, index_hbm, label_hbm, place_ref, meta_ref, given, sems):
    loads = [
        pltpu.make_async_copy(source, given.at[pl.ds(i, 1)], sems.at[i])
        for i, source in enumerate((bucket_hbm, index_hbm, label_hbm))
    ]
    for load in loads:
        load.start()
    width = 2 * LANES
    chunks = FACTS_HERE // width
    upto = jnp.where(
        lax.broadcasted_iota(jnp.int32, (width, width), 0)
        <= lax.broadcasted_iota(jnp.int32, (width, width), 1),
        1.0,
        0.0,
    ).astype(bf16)
    for load in loads:
        load.wait()
    bucket = given[0:1, :]
    owner = (bucket >> 1) + ((bucket & 1) ^ core_ref[0]) * CHIPS
    label = given[2:3, :]
    owner_hits = onehot(owner, OWNERS)
    stack = jnp.concatenate(
        [owner_hits[:, c * width : (c + 1) * width] for c in range(chunks)], 0
    )
    prefix = dot_nn(stack, upto)
    before = jnp.zeros((OWNERS, 1), f32)
    ranks = []
    for c in range(chunks):
        here = prefix[c * OWNERS : (c + 1) * OWNERS]
        mine = hits(owner[:, c * width : (c + 1) * width], OWNERS)
        ranks.append(jnp.sum(jnp.where(mine, here + before, 0.0), 0, keepdims=True))
        before = before + here[:, width - 1 : width]
    rank = jnp.concatenate(ranks, 1).astype(jnp.int32) - 1
    place_ref[...] = rank + (owner << OWNER_BIT) + (label << LABEL_BIT)
    index = given[1:2, :]
    low = (index & (LANES - 1)).astype(f32)
    high = ((index >> 7) + (label << (LABEL_BIT - 7)) + (1 << (VALID_BIT - 7))).astype(f32)
    mine = hits(owner, OWNERS)
    fields = jnp.concatenate([jnp.where(mine, low, 0.0), jnp.where(mine, high, 0.0)], 0)
    packed = dot_nt(fields.astype(bf16), onehot(rank, LANES))
    meta_ref[...] = packed[:OWNERS] + packed[OWNERS:] * LANES


def places(place_ref):
    place = place_ref[...]
    return place & (LANES - 1), (place >> OWNER_BIT) & (OWNERS - 1), place >> LABEL_BIT


def pack_kernel(recv_ref, place_ref, meta_ref, out_ref, dims_ref, facts_ref, left_ref):
    total = recv_ref[0]
    for peer in range(1, PEERS):
        total = total + recv_ref[peer]
    dims_ref[...] = total[:DIM_ROWS]
    rank, owner, _ = places(place_ref)
    for i in range(FACT_ROWS):
        cut = slice(i * LANES, (i + 1) * LANES)
        mine = hits(owner[:, cut], OWNERS)
        for part, value in enumerate(split3(total[DIM_ROWS + i : DIM_ROWS + i + 1])):
            left_ref[part * OWNERS : (part + 1) * OWNERS, cut] = jnp.where(mine, value, 0.0).astype(bf16)
    packed = dot_nt(left_ref[...], onehot(rank, LANES))
    packed = packed[:OWNERS] + packed[OWNERS : 2 * OWNERS] + packed[2 * OWNERS :]
    facts_ref[...] = packed
    for chip in range(CHIPS):
        out_ref[chip, :DIM_ROWS, :] = total[:DIM_ROWS]
        for other in range(2):
            row, slot = DIM_ROWS + other, other * CHIPS + chip
            out_ref[chip, row : row + 1, :] = packed[slot : slot + 1]
            out_ref[chip, row + 2 : row + 3, :] = meta_ref[slot : slot + 1, :]


def stacked(value):
    return jnp.concatenate(split3(value), 0).astype(bf16)


def found(parts, row):
    count = parts.shape[0] // 3
    value = parts[:count] + parts[count : 2 * count] + parts[2 * count :]
    return jnp.sum(jnp.where(hits(row, count), value, 0.0), 0, keepdims=True)


def sigmoid(value):
    return 1.0 / (1.0 + jnp.exp(-value))


def half(other, recv_ref, dims_ref, facts_ref, meta_ref, place_ref, scratch):
    home_ref, own_ref, code_ref, low_ref, left_ref = scratch
    slots = slice(other * CHIPS, (other + 1) * CHIPS)
    meta = meta_ref[slots, :].astype(jnp.int32)
    dims = stacked(dims_ref[...])
    for chip in range(CHIPS):
        code = meta[chip : chip + 1]
        parts = dot_nn(stacked(recv_ref[chip, :DIM_ROWS, :]), onehot(code & (LANES - 1), LANES))
        home_ref[chip : chip + 1, :] = found(parts, (code >> 7) & (DIM_ROWS - 1))
        row = DIM_ROWS + other
        cut = slice(chip * LANES, (chip + 1) * LANES)
        code = recv_ref[chip, row + 2 : row + 3, :].astype(jnp.int32)
        code_ref[chip : chip + 1, :] = code
        column = onehot(code & (LANES - 1), LANES)
        low_ref[:, cut] = column
        own_ref[chip : chip + 1, :] = recv_ref[chip, row : row + 1, :] + found(
            dot_nn(dims, column), (code >> 7) & (DIM_ROWS - 1)
        )
    rank, owner, _ = places(place_ref)
    prob = sigmoid(home_ref[...] + facts_ref[slots, :])
    prob = found(dot_nn(stacked(prob), onehot(rank, LANES)), owner - other * CHIPS)
    code = code_ref[...]
    residual = (sigmoid(own_ref[...]) - ((code >> LABEL_BIT) & 1).astype(f32)) * (
        code >> VALID_BIT
    ).astype(f32)
    terms = split3(residual)
    for chip in range(CHIPS):
        cut = slice(chip * LANES, (chip + 1) * LANES)
        mine = hits((code[chip : chip + 1] >> 7) & (DIM_ROWS - 1), DIM_ROWS)
        for part, value in enumerate(terms):
            left_ref[part * DIM_ROWS : (part + 1) * DIM_ROWS, cut] = jnp.where(
                mine, value[chip : chip + 1], 0.0
            ).astype(bf16)
    sums = dot_nt(left_ref[...], low_ref[...])
    return prob, sums[:DIM_ROWS] + sums[DIM_ROWS : 2 * DIM_ROWS] + sums[2 * DIM_ROWS :]


def same_core_kernel(
    recv_ref, dims_ref, facts_ref, meta_ref, place_ref, prob_ref, sums_ref, *scratch
):
    prob_ref[...], sums_ref[...] = half(
        0, recv_ref, dims_ref, facts_ref, meta_ref, place_ref, scratch
    )


def grads_kernel(
    recv_ref,
    dims_ref,
    facts_ref,
    meta_ref,
    place_ref,
    prob_half_ref,
    sums_half_ref,
    fact_ref,
    dim_ref,
    out_ref,
    prob_ref,
    *scratch,
):
    prob, sums = half(1, recv_ref, dims_ref, facts_ref, meta_ref, place_ref, scratch)
    prob = prob + prob_half_ref[...]
    sums = sums + sums_half_ref[...]
    prob_ref[...] = prob
    residual = prob - places(place_ref)[2].astype(f32)
    grad_fact = jnp.sum(dot_nn(stacked_row(residual), fact_ref[...]), 0, keepdims=True)
    rows = jnp.concatenate([stacked_row(sums[i : i + 1]) for i in range(DIM_ROWS)], 1)
    grad_dim = jnp.sum(dot_nn(rows, dim_ref[...]), 0, keepdims=True)
    for owner in range(OWNERS):
        out_ref[owner, 0:1, :] = grad_fact
        out_ref[owner, 1:2, :] = grad_dim


def update_kernel(recv_ref, fact_weight_ref, dim_weight_ref, fact_out_ref, dim_out_ref):
    total = recv_ref[0]
    for peer in range(1, OWNERS):
        total = total + recv_ref[peer]
    scale = 0.5 / (OWNERS * FACTS_HERE) ** 0.5
    fact_out_ref[...] = fact_weight_ref[...] - scale * total[0:1]
    dim_out_ref[...] = dim_weight_ref[...] - scale * total[1:2]


HALF_SCRATCH = [
    pltpu.VMEM((CHIPS, LANES), f32),
    pltpu.VMEM((CHIPS, LANES), f32),
    pltpu.VMEM((CHIPS, LANES), jnp.int32),
    pltpu.VMEM((LANES, CHIPS * LANES), bf16),
    pltpu.VMEM((3 * DIM_ROWS, CHIPS * LANES), bf16),
]


def call(kernel, outs, scratch=(), in_specs=None, flops=None, vmem=32 << 20):
    extra = {} if in_specs is None else {"in_specs": in_specs}
    if flops is not None:
        extra["cost_estimate"] = pl.CostEstimate(
            flops=flops, bytes_accessed=1 << 20, transcendentals=0
        )
    return pl.pallas_call(
        kernel,
        out_shape=[jax.ShapeDtypeStruct(shape, dtype) for shape, dtype in outs],
        scratch_shapes=list(scratch),
        compiler_params=pltpu.CompilerParams(vmem_limit_bytes=vmem),
        **extra,
    )


def exchange(value, axis, groups=None):
    return lax.all_to_all(
        value, axis, split_axis=0, concat_axis=0, tiled=True, axis_index_groups=groups
    )


def shards(fact_table, dim_table, fact_weight, dim_weight, bucket, row_index, labels):
    bucket = bucket.reshape(1, FACTS_HERE)
    row_index = row_index.reshape(1, FACTS_HERE)
    labels = labels.reshape(1, FACTS_HERE)
    fact_weight = fact_weight.reshape(1, LANES)
    dim_weight = dim_weight.reshape(1, LANES)
    core = (lax.axis_index("rows") & 1).reshape(1)
    in_hbm = pl.BlockSpec(memory_space=pltpu.HBM)

    (partial,) = call(
        scores_kernel,
        [((PEERS, SCORE_ROWS, LANES), f32)],
        [
            pltpu.VMEM(fact_table.shape, bf16),
            pltpu.VMEM(dim_table.shape, bf16),
            pltpu.VMEM((2, LANES), f32),
            pltpu.SemaphoreType.DMA((2 + (len(fact_table) + len(dim_table)) // PIECE,)),
        ],
        [in_hbm] * 4,
        vmem=(63 << 20) + (1 << 19),
    )(fact_table, dim_table, fact_weight, dim_weight)
    place, meta = call(
        slots_kernel,
        [((1, FACTS_HERE), jnp.int32), ((OWNERS, LANES), f32)],
        [pltpu.VMEM((3, FACTS_HERE), jnp.int32), pltpu.SemaphoreType.DMA((3,))],
        [pl.BlockSpec(memory_space=pltpu.SMEM)] + [in_hbm] * 3,
    )(core, bucket, row_index, labels)
    partial = exchange(partial, "feat")
    blocks, dims, facts = call(
        pack_kernel,
        [((CHIPS, BLOCK_ROWS, LANES), f32), ((DIM_ROWS, LANES), f32), ((OWNERS, LANES), f32)],
        [pltpu.VMEM((3 * OWNERS, FACTS_HERE), bf16)],
    )(partial, place, meta)
    blocks = exchange(
        blocks, "rows", [[2 * chip + core for chip in range(CHIPS)] for core in range(2)]
    )
    other_blocks = lax.ppermute(blocks, "rows", [(i, i ^ 1) for i in range(OWNERS)])
    prob_half, sums_half = call(
        same_core_kernel,
        [((1, FACTS_HERE), f32), ((DIM_ROWS, LANES), f32)],
        HALF_SCRATCH,
        flops=1 << 31,
    )(blocks, dims, facts, meta, place)
    grads, prob = call(
        grads_kernel,
        [((OWNERS, 2, LANES), f32), ((1, FACTS_HERE), f32)],
        HALF_SCRATCH,
    )(other_blocks, dims, facts, meta, place, prob_half, sums_half, fact_table, dim_table)
    grads = exchange(grads, "rows")
    new_fact, new_dim = call(update_kernel, [((1, LANES), f32), ((1, LANES), f32)])(
        grads, fact_weight, dim_weight
    )
    return new_fact.reshape(-1), new_dim.reshape(-1), prob.reshape(-1)


def solution(mesh):
    return jax.shard_map(
        shards,
        mesh=mesh,
        in_specs=(
            P("rows", "feat"),
            P("rows", "feat"),
            P("feat"),
            P("feat"),
            P("rows", None),
            P("rows"),
            P("rows"),
        ),
        out_specs=(P("feat"), P("feat"), P("rows")),
        check_vma=False,
    )
```

```python
import jax
import jax.numpy as jnp
from jax import lax
from jax.experimental import pallas as pl
from jax.experimental.pallas import tpu as pltpu
from jax.sharding import PartitionSpec as P

LANES = 128
OWNERS = 32
CHIPS = 16
PEERS = 8
DIM_ROWS = 32
FACT_ROWS = 16
FACTS_HERE = FACT_ROWS * LANES
SCORE_ROWS = DIM_ROWS + FACT_ROWS
BLOCK_ROWS = DIM_ROWS + 4
PIECE = 2048
LABEL_BIT = 12
VALID_BIT = 13

bf16 = jnp.bfloat16
f32 = jnp.float32


def split3(value):
    high = value.astype(bf16).astype(f32)
    rest = value - high
    middle = rest.astype(bf16).astype(f32)
    return high, middle, rest - middle


def stacked_row(row):
    shape = (8, row.shape[1])
    place = lax.broadcasted_iota(jnp.int32, shape, 0)
    high, middle, low = split3(row)
    return jnp.where(
        place == 0, high, jnp.where(place == 1, middle, jnp.where(place == 2, low, 0.0))
    ).astype(bf16)


def dot_nt(left, right):
    return lax.dot_general(
        left, right, (((1,), (1,)), ((), ())), preferred_element_type=f32
    )


def dot_nn(left, right):
    return jnp.dot(left, right, preferred_element_type=f32)


def hits(row, count):
    return lax.broadcasted_iota(jnp.int32, (count, row.shape[1]), 0) == row


def onehot(row, count):
    return jnp.where(hits(row, count), 1.0, 0.0).astype(bf16)


def scores_kernel(
    fact_hbm, dim_hbm, fact_weight_hbm, dim_weight_hbm, out_ref, fact, dim, weights, sems
):
    def copies(source, target, first):
        found = []
        for i in range(source.shape[0] // PIECE):
            cut = pl.ds(i * PIECE, PIECE)
            found.append(pltpu.make_async_copy(source.at[cut], target.at[cut], sems.at[first + i]))
        return found

    dim_pieces = copies(dim_hbm, dim, 2)
    fact_pieces = copies(fact_hbm, fact, 2 + len(dim_pieces))
    dim_weight = pltpu.make_async_copy(dim_weight_hbm, weights.at[pl.ds(0, 1)], sems.at[0])
    fact_weight = pltpu.make_async_copy(fact_weight_hbm, weights.at[pl.ds(1, 1)], sems.at[1])
    for copy in [dim_weight, fact_weight] + fact_pieces + dim_pieces:
        copy.start()
    for row, place, weight, table, pieces in (
        (DIM_ROWS, 1, fact_weight, fact, fact_pieces),
        (0, 0, dim_weight, dim, dim_pieces),
    ):
        weight.wait()
        for piece in pieces:
            piece.wait()
        part = dot_nt(stacked_row(weights[place : place + 1, :]), table[...])
        part = jnp.sum(part, 0, keepdims=True)
        for i in range(table.shape[0] // LANES):
            out_ref[0, row : row + 1, :] = part[:, i * LANES : (i + 1) * LANES]
            row += 1
    for peer in range(1, PEERS):
        out_ref[peer] = out_ref[0]


def slots_kernel(
    core_ref,
    bucket_hbm,
    index_hbm,
    label_hbm,
    place_ref,
    meta_ref,
    rank_hits_ref,
    row_hits_ref,
    given,
    sems,
):
    loads = [
        pltpu.make_async_copy(source, given.at[pl.ds(i, 1)], sems.at[i])
        for i, source in enumerate((bucket_hbm, index_hbm, label_hbm))
    ]
    for load in loads:
        load.start()
    width = 2 * LANES
    chunks = FACTS_HERE // width
    upto = jnp.where(
        lax.broadcasted_iota(jnp.int32, (width, width), 0)
        <= lax.broadcasted_iota(jnp.int32, (width, width), 1),
        1.0,
        0.0,
    ).astype(bf16)
    for load in loads:
        load.wait()
    bucket = given[0:1, :]
    owner = (bucket >> 1) + ((bucket & 1) ^ core_ref[0]) * CHIPS
    label = given[2:3, :]
    owner_hits = onehot(owner, OWNERS)
    stack = jnp.concatenate(
        [owner_hits[:, c * width : (c + 1) * width] for c in range(chunks)], 0
    )
    prefix = dot_nn(stack, upto)
    before = jnp.zeros((OWNERS, 1), f32)
    ranks = []
    for c in range(chunks):
        here = prefix[c * OWNERS : (c + 1) * OWNERS]
        mine = hits(owner[:, c * width : (c + 1) * width], OWNERS)
        ranks.append(jnp.sum(jnp.where(mine, here + before, 0.0), 0, keepdims=True))
        before = before + here[:, width - 1 : width]
    rank = jnp.concatenate(ranks, 1).astype(jnp.int32) - 1
    place_ref[...] = owner + (label << LABEL_BIT)
    index = given[1:2, :]
    low = (index & (LANES - 1)).astype(f32)
    high = ((index >> 7) + (label << (LABEL_BIT - 7)) + (1 << (VALID_BIT - 7))).astype(f32)
    mine = hits(owner, OWNERS)
    fields = jnp.concatenate([jnp.where(mine, low, 0.0), jnp.where(mine, high, 0.0)], 0)
    rank_hits = onehot(rank, LANES)
    rank_hits_ref[...] = rank_hits
    packed = dot_nt(fields.astype(bf16), rank_hits)
    meta_ref[...] = packed[:OWNERS] + packed[OWNERS:] * LANES
    low = packed[:OWNERS].astype(jnp.int32)
    for owner in range(OWNERS):
        cut = slice(owner * LANES, (owner + 1) * LANES)
        row_hits_ref[:, cut] = onehot(low[owner : owner + 1], LANES)


def places(place_ref):
    place = place_ref[...]
    return place & (OWNERS - 1), place >> LABEL_BIT


def pack_kernel(
    recv_ref, place_ref, meta_ref, rank_hits_ref, out_ref, dims_ref, facts_ref, left_ref
):
    total = recv_ref[0]
    for peer in range(1, PEERS):
        total = total + recv_ref[peer]
    dims_ref[...] = total[:DIM_ROWS]
    owner, _ = places(place_ref)
    for i in range(FACT_ROWS):
        cut = slice(i * LANES, (i + 1) * LANES)
        mine = hits(owner[:, cut], OWNERS)
        for part, value in enumerate(split3(total[DIM_ROWS + i : DIM_ROWS + i + 1])):
            left_ref[part * OWNERS : (part + 1) * OWNERS, cut] = jnp.where(mine, value, 0.0).astype(bf16)
    packed = dot_nt(left_ref[...], rank_hits_ref[...])
    packed = packed[:OWNERS] + packed[OWNERS : 2 * OWNERS] + packed[2 * OWNERS :]
    facts_ref[...] = packed
    for chip in range(CHIPS):
        out_ref[chip, :DIM_ROWS, :] = total[:DIM_ROWS]
        for other in range(2):
            row, slot = DIM_ROWS + other, other * CHIPS + chip
            out_ref[chip, row : row + 1, :] = packed[slot : slot + 1]
            out_ref[chip, row + 2 : row + 3, :] = meta_ref[slot : slot + 1, :]


def stacked(value, count=3):
    return jnp.concatenate(split3(value)[:count], 0).astype(bf16)


def summed(parts, count):
    total = parts[:count]
    for start in range(count, parts.shape[0], count):
        total = total + parts[start : start + count]
    return total


def taken(value, row):
    return jnp.sum(jnp.where(hits(row, value.shape[0]), value, 0.0), 0, keepdims=True)


def sigmoid(value):
    return 1.0 / (1.0 + jnp.exp(-value))


def half(
    other, recv_ref, dims_ref, facts_ref, meta_ref, place_ref, rank_hits_ref, row_hits_ref, scratch
):
    home_ref, own_ref, code_ref, low_ref, left_ref = scratch
    slots = slice(other * CHIPS, (other + 1) * CHIPS)
    meta = meta_ref[slots, :].astype(jnp.int32)
    dims = stacked(dims_ref[...])
    for chip in range(CHIPS):
        cut = slice((other * CHIPS + chip) * LANES, (other * CHIPS + chip + 1) * LANES)
        parts = dot_nn(stacked(recv_ref[chip, :DIM_ROWS, :]), row_hits_ref[:, cut])
        home_ref[chip : chip + 1, :] = taken(
            summed(parts, DIM_ROWS), (meta[chip : chip + 1] >> 7) & (DIM_ROWS - 1)
        )
        row = DIM_ROWS + other
        cut = slice(chip * LANES, (chip + 1) * LANES)
        code = recv_ref[chip, row + 2 : row + 3, :].astype(jnp.int32)
        code_ref[chip : chip + 1, :] = code
        column = onehot(code & (LANES - 1), LANES)
        low_ref[:, cut] = column
        own_ref[chip : chip + 1, :] = recv_ref[chip, row : row + 1, :] + taken(
            summed(dot_nn(dims, column), DIM_ROWS), (code >> 7) & (DIM_ROWS - 1)
        )
    prob = stacked(sigmoid(home_ref[...] + facts_ref[slots, :]), 2)
    prob = taken(
        summed(dot_nn(prob, rank_hits_ref[...]), CHIPS), places(place_ref)[0] - other * CHIPS
    )
    code = code_ref[...]
    residual = (sigmoid(own_ref[...]) - ((code >> LABEL_BIT) & 1).astype(f32)) * (
        code >> VALID_BIT
    ).astype(f32)
    terms = split3(residual)[:2]
    for chip in range(CHIPS):
        cut = slice(chip * LANES, (chip + 1) * LANES)
        mine = hits((code[chip : chip + 1] >> 7) & (DIM_ROWS - 1), DIM_ROWS)
        for part, value in enumerate(terms):
            left_ref[part * DIM_ROWS : (part + 1) * DIM_ROWS, cut] = jnp.where(
                mine, value[chip : chip + 1], 0.0
            ).astype(bf16)
    return prob, summed(dot_nt(left_ref[...], low_ref[...]), DIM_ROWS)


def same_core_kernel(
    recv_ref,
    dims_ref,
    facts_ref,
    meta_ref,
    place_ref,
    rank_hits_ref,
    row_hits_ref,
    prob_ref,
    sums_ref,
    *scratch,
):
    prob_ref[...], sums_ref[...] = half(
        0, recv_ref, dims_ref, facts_ref, meta_ref, place_ref, rank_hits_ref, row_hits_ref, scratch
    )


def grads_kernel(
    recv_ref,
    dims_ref,
    facts_ref,
    meta_ref,
    place_ref,
    rank_hits_ref,
    row_hits_ref,
    prob_half_ref,
    sums_half_ref,
    fact_ref,
    dim_ref,
    out_ref,
    prob_ref,
    *scratch,
):
    prob, sums = half(
        1, recv_ref, dims_ref, facts_ref, meta_ref, place_ref, rank_hits_ref, row_hits_ref, scratch
    )
    prob = prob + prob_half_ref[...]
    sums = sums + sums_half_ref[...]
    prob_ref[...] = prob
    residual = prob - places(place_ref)[1].astype(f32)
    grad_fact = jnp.sum(dot_nn(stacked_row(residual), fact_ref[...]), 0, keepdims=True)
    rows = jnp.concatenate([stacked_row(sums[i : i + 1]) for i in range(DIM_ROWS)], 1)
    side = DIM_ROWS // 2 * LANES
    both = dot_nn(
        jnp.concatenate([rows[:, :side], rows[:, side:]], 0),
        jnp.concatenate([dim_ref[:side, :], dim_ref[side:, :]], 1),
    )
    grad_dim = jnp.sum(both[:8, :LANES] + both[8:, LANES:], 0, keepdims=True)
    for owner in range(OWNERS):
        out_ref[owner, 0:1, :] = grad_fact
        out_ref[owner, 1:2, :] = grad_dim


def update_kernel(recv_ref, fact_weight_ref, dim_weight_ref, fact_out_ref, dim_out_ref):
    total = recv_ref[0]
    for peer in range(1, OWNERS):
        total = total + recv_ref[peer]
    scale = 0.5 / (OWNERS * FACTS_HERE) ** 0.5
    fact_out_ref[...] = fact_weight_ref[...] - scale * total[0:1]
    dim_out_ref[...] = dim_weight_ref[...] - scale * total[1:2]


HALF_SCRATCH = [
    pltpu.VMEM((CHIPS, LANES), f32),
    pltpu.VMEM((CHIPS, LANES), f32),
    pltpu.VMEM((CHIPS, LANES), jnp.int32),
    pltpu.VMEM((LANES, CHIPS * LANES), bf16),
    pltpu.VMEM((2 * DIM_ROWS, CHIPS * LANES), bf16),
]


def call(kernel, outs, scratch=(), in_specs=None, flops=None, vmem=32 << 20):
    extra = {} if in_specs is None else {"in_specs": in_specs}
    if flops is not None:
        extra["cost_estimate"] = pl.CostEstimate(
            flops=flops, bytes_accessed=1 << 20, transcendentals=0
        )
    return pl.pallas_call(
        kernel,
        name=kernel.__name__,
        out_shape=[jax.ShapeDtypeStruct(shape, dtype) for shape, dtype in outs],
        scratch_shapes=list(scratch),
        compiler_params=pltpu.CompilerParams(vmem_limit_bytes=vmem),
        **extra,
    )


def exchange(value, axis, groups=None):
    return lax.all_to_all(
        value, axis, split_axis=0, concat_axis=0, tiled=True, axis_index_groups=groups
    )


def shards(fact_table, dim_table, fact_weight, dim_weight, bucket, row_index, labels):
    bucket = bucket.reshape(1, FACTS_HERE)
    row_index = row_index.reshape(1, FACTS_HERE)
    labels = labels.reshape(1, FACTS_HERE)
    fact_weight = fact_weight.reshape(1, LANES)
    dim_weight = dim_weight.reshape(1, LANES)
    core = (lax.axis_index("rows") & 1).reshape(1)
    in_hbm = pl.BlockSpec(memory_space=pltpu.HBM)

    (partial,) = call(
        scores_kernel,
        [((PEERS, SCORE_ROWS, LANES), f32)],
        [
            pltpu.VMEM(fact_table.shape, bf16),
            pltpu.VMEM(dim_table.shape, bf16),
            pltpu.VMEM((2, LANES), f32),
            pltpu.SemaphoreType.DMA((2 + (len(fact_table) + len(dim_table)) // PIECE,)),
        ],
        [in_hbm] * 4,
        vmem=(53 << 20) + (1 << 19),
    )(fact_table, dim_table, fact_weight, dim_weight)
    place, meta, rank_hits, row_hits = call(
        slots_kernel,
        [
            ((1, FACTS_HERE), jnp.int32),
            ((OWNERS, LANES), f32),
            ((LANES, FACTS_HERE), bf16),
            ((LANES, OWNERS * LANES), bf16),
        ],
        [pltpu.VMEM((3, FACTS_HERE), jnp.int32), pltpu.SemaphoreType.DMA((3,))],
        [pl.BlockSpec(memory_space=pltpu.SMEM)] + [in_hbm] * 3,
    )(core, bucket, row_index, labels)
    partial = exchange(partial, "feat")
    blocks, dims, facts = call(
        pack_kernel,
        [((CHIPS, BLOCK_ROWS, LANES), f32), ((DIM_ROWS, LANES), f32), ((OWNERS, LANES), f32)],
        [pltpu.VMEM((3 * OWNERS, FACTS_HERE), bf16)],
    )(partial, place, meta, rank_hits)
    blocks = exchange(
        blocks, "rows", [[2 * chip + core for chip in range(CHIPS)] for core in range(2)]
    )
    other_blocks = lax.ppermute(blocks, "rows", [(i, i ^ 1) for i in range(OWNERS)])
    prob_half, sums_half = call(
        same_core_kernel,
        [((1, FACTS_HERE), f32), ((DIM_ROWS, LANES), f32)],
        HALF_SCRATCH,
        flops=1 << 31,
    )(blocks, dims, facts, meta, place, rank_hits, row_hits)
    grads, prob = call(
        grads_kernel,
        [((OWNERS, 2, LANES), f32), ((1, FACTS_HERE), f32)],
        HALF_SCRATCH,
    )(
        other_blocks,
        dims,
        facts,
        meta,
        place,
        rank_hits,
        row_hits,
        prob_half,
        sums_half,
        fact_table,
        dim_table,
    )
    grads = exchange(grads, "rows")
    new_fact, new_dim = call(update_kernel, [((1, LANES), f32), ((1, LANES), f32)])(
        grads, fact_weight, dim_weight
    )
    return new_fact.reshape(-1), new_dim.reshape(-1), prob.reshape(-1)


def solution(mesh):
    return jax.shard_map(
        shards,
        mesh=mesh,
        in_specs=(
            P("rows", "feat"),
            P("rows", "feat"),
            P("feat"),
            P("feat"),
            P("rows", None),
            P("rows"),
            P("rows"),
        ),
        out_specs=(P("feat"), P("feat"), P("rows")),
        check_vma=False,
    )
```

```python
import jax
import jax.numpy as jnp
from jax import lax
from jax.experimental import pallas as pl
from jax.experimental.pallas import tpu as pltpu
from jax.sharding import PartitionSpec as P

LANES = 128
OWNERS = 32
CHIPS = 16
PEERS = 8
DIM_ROWS = 32
FACT_ROWS = 16
FACTS_HERE = FACT_ROWS * LANES
SCORE_ROWS = DIM_ROWS + FACT_ROWS
BLOCK_ROWS = DIM_ROWS + 4
PIECE = 2048
LABEL_BIT = 12
VALID_BIT = 13

bf16 = jnp.bfloat16
f32 = jnp.float32


def split3(value):
    high = value.astype(bf16).astype(f32)
    rest = value - high
    middle = rest.astype(bf16).astype(f32)
    return high, middle, rest - middle


def stacked_row(row):
    shape = (8, row.shape[1])
    place = lax.broadcasted_iota(jnp.int32, shape, 0)
    high, middle, low = split3(row)
    return jnp.where(
        place == 0, high, jnp.where(place == 1, middle, jnp.where(place == 2, low, 0.0))
    ).astype(bf16)


def dot_nt(left, right):
    return lax.dot_general(
        left, right, (((1,), (1,)), ((), ())), preferred_element_type=f32
    )


def dot_nn(left, right):
    return jnp.dot(left, right, preferred_element_type=f32)


def hits(row, count):
    return lax.broadcasted_iota(jnp.int32, (count, row.shape[1]), 0) == row


def onehot(row, count):
    return jnp.where(hits(row, count), 1.0, 0.0).astype(bf16)


def scores_kernel(
    fact_hbm, dim_hbm, fact_weight_hbm, dim_weight_hbm, out_ref, fact, dim, weights, sems
):
    def copies(source, target, first):
        found = []
        for i in range(source.shape[0] // PIECE):
            cut = pl.ds(i * PIECE, PIECE)
            found.append(pltpu.make_async_copy(source.at[cut], target.at[cut], sems.at[first + i]))
        return found

    dim_pieces = copies(dim_hbm, dim, 2)
    fact_pieces = copies(fact_hbm, fact, 2 + len(dim_pieces))
    dim_weight = pltpu.make_async_copy(dim_weight_hbm, weights.at[pl.ds(0, 1)], sems.at[0])
    fact_weight = pltpu.make_async_copy(fact_weight_hbm, weights.at[pl.ds(1, 1)], sems.at[1])
    for copy in [dim_weight, fact_weight] + fact_pieces + dim_pieces:
        copy.start()
    for row, place, weight, table, pieces in (
        (DIM_ROWS, 1, fact_weight, fact, fact_pieces),
        (0, 0, dim_weight, dim, dim_pieces),
    ):
        weight.wait()
        for piece in pieces:
            piece.wait()
        part = dot_nt(stacked_row(weights[place : place + 1, :]), table[...])
        part = jnp.sum(part, 0, keepdims=True)
        for i in range(table.shape[0] // LANES):
            out_ref[0, row : row + 1, :] = part[:, i * LANES : (i + 1) * LANES]
            row += 1
    for peer in range(1, PEERS):
        out_ref[peer] = out_ref[0]


def slots_kernel(
    core_ref,
    bucket_hbm,
    index_hbm,
    label_hbm,
    place_ref,
    meta_ref,
    rank_hits_ref,
    row_hits_ref,
    given,
    sems,
):
    loads = [
        pltpu.make_async_copy(source, given.at[pl.ds(i, 1)], sems.at[i])
        for i, source in enumerate((bucket_hbm, index_hbm, label_hbm))
    ]
    for load in loads:
        load.start()
    width = 2 * LANES
    chunks = FACTS_HERE // width
    upto = jnp.where(
        lax.broadcasted_iota(jnp.int32, (width, width), 0)
        <= lax.broadcasted_iota(jnp.int32, (width, width), 1),
        1.0,
        0.0,
    ).astype(bf16)
    for load in loads:
        load.wait()
    bucket = given[0:1, :]
    owner = (bucket >> 1) + ((bucket & 1) ^ core_ref[0]) * CHIPS
    label = given[2:3, :]
    owner_hits = onehot(owner, OWNERS)
    stack = jnp.concatenate(
        [owner_hits[:, c * width : (c + 1) * width] for c in range(chunks)], 0
    )
    prefix = dot_nn(stack, upto)
    before = jnp.zeros((OWNERS, 1), f32)
    ranks = []
    for c in range(chunks):
        here = prefix[c * OWNERS : (c + 1) * OWNERS]
        mine = hits(owner[:, c * width : (c + 1) * width], OWNERS)
        ranks.append(jnp.sum(jnp.where(mine, here + before, 0.0), 0, keepdims=True))
        before = before + here[:, width - 1 : width]
    rank = jnp.concatenate(ranks, 1).astype(jnp.int32) - 1
    place_ref[...] = owner + (label << LABEL_BIT)
    index = given[1:2, :]
    low = (index & (LANES - 1)).astype(f32)
    high = ((index >> 7) + (label << (LABEL_BIT - 7)) + (1 << (VALID_BIT - 7))).astype(f32)
    mine = hits(owner, OWNERS)
    fields = jnp.concatenate([jnp.where(mine, low, 0.0), jnp.where(mine, high, 0.0)], 0)
    rank_hits = onehot(rank, LANES)
    rank_hits_ref[...] = rank_hits
    packed = dot_nt(fields.astype(bf16), rank_hits)
    meta_ref[...] = packed[:OWNERS] + packed[OWNERS:] * LANES
    low = packed[:OWNERS].astype(jnp.int32)
    for owner in range(OWNERS):
        cut = slice(owner * LANES, (owner + 1) * LANES)
        row_hits_ref[:, cut] = onehot(low[owner : owner + 1], LANES)


def places(place_ref):
    place = place_ref[...]
    return place & (OWNERS - 1), place >> LABEL_BIT


def pack_kernel(
    recv_ref, place_ref, meta_ref, rank_hits_ref, out_ref, dims_ref, facts_ref, left_ref
):
    total = recv_ref[0]
    for peer in range(1, PEERS):
        total = total + recv_ref[peer]
    dims_ref[...] = total[:DIM_ROWS]
    owner, _ = places(place_ref)
    for i in range(FACT_ROWS):
        cut = slice(i * LANES, (i + 1) * LANES)
        mine = hits(owner[:, cut], OWNERS)
        for part, value in enumerate(split3(total[DIM_ROWS + i : DIM_ROWS + i + 1])):
            left_ref[part * OWNERS : (part + 1) * OWNERS, cut] = jnp.where(mine, value, 0.0).astype(bf16)
    packed = dot_nt(left_ref[...], rank_hits_ref[...])
    packed = packed[:OWNERS] + packed[OWNERS : 2 * OWNERS] + packed[2 * OWNERS :]
    facts_ref[...] = packed
    for chip in range(CHIPS):
        out_ref[chip, :DIM_ROWS, :] = total[:DIM_ROWS]
        for other in range(2):
            row, slot = DIM_ROWS + other, other * CHIPS + chip
            out_ref[chip, row : row + 1, :] = packed[slot : slot + 1]
            out_ref[chip, row + 2 : row + 3, :] = meta_ref[slot : slot + 1, :]


def stacked(value, count=3):
    return jnp.concatenate(split3(value)[:count], 0).astype(bf16)


def summed(parts, count):
    total = parts[:count]
    for start in range(count, parts.shape[0], count):
        total = total + parts[start : start + count]
    return total


def taken(value, row):
    return jnp.sum(jnp.where(hits(row, value.shape[0]), value, 0.0), 0, keepdims=True)


def sigmoid(value):
    return 1.0 / (1.0 + jnp.exp(-value))


def half(
    other, recv_ref, dims_ref, facts_ref, meta_ref, place_ref, rank_hits_ref, row_hits_ref, scratch
):
    home_ref, own_ref, code_ref, low_ref, left_ref = scratch
    slots = slice(other * CHIPS, (other + 1) * CHIPS)
    meta = meta_ref[slots, :].astype(jnp.int32)
    dims = stacked(dims_ref[...])
    for chip in range(CHIPS):
        cut = slice((other * CHIPS + chip) * LANES, (other * CHIPS + chip + 1) * LANES)
        parts = dot_nn(stacked(recv_ref[chip, :DIM_ROWS, :]), row_hits_ref[:, cut])
        home_ref[chip : chip + 1, :] = taken(
            summed(parts, DIM_ROWS), (meta[chip : chip + 1] >> 7) & (DIM_ROWS - 1)
        )
        row = DIM_ROWS + other
        cut = slice(chip * LANES, (chip + 1) * LANES)
        code = recv_ref[chip, row + 2 : row + 3, :].astype(jnp.int32)
        code_ref[chip : chip + 1, :] = code
        column = onehot(code & (LANES - 1), LANES)
        low_ref[:, cut] = column
        own_ref[chip : chip + 1, :] = recv_ref[chip, row : row + 1, :] + taken(
            summed(dot_nn(dims, column), DIM_ROWS), (code >> 7) & (DIM_ROWS - 1)
        )
    prob = stacked(sigmoid(home_ref[...] + facts_ref[slots, :]), 2)
    prob = taken(
        summed(dot_nn(prob, rank_hits_ref[...]), CHIPS), places(place_ref)[0] - other * CHIPS
    )
    code = code_ref[...]
    residual = (sigmoid(own_ref[...]) - ((code >> LABEL_BIT) & 1).astype(f32)) * (
        code >> VALID_BIT
    ).astype(f32)
    terms = split3(residual)[:2]
    for chip in range(CHIPS):
        cut = slice(chip * LANES, (chip + 1) * LANES)
        mine = hits((code[chip : chip + 1] >> 7) & (DIM_ROWS - 1), DIM_ROWS)
        for part, value in enumerate(terms):
            left_ref[part * DIM_ROWS : (part + 1) * DIM_ROWS, cut] = jnp.where(
                mine, value[chip : chip + 1], 0.0
            ).astype(bf16)
    return prob, summed(dot_nt(left_ref[...], low_ref[...]), DIM_ROWS)


def same_core_kernel(
    recv_ref,
    dims_ref,
    facts_ref,
    meta_ref,
    place_ref,
    rank_hits_ref,
    row_hits_ref,
    prob_ref,
    sums_ref,
    *scratch,
):
    prob_ref[...], sums_ref[...] = half(
        0, recv_ref, dims_ref, facts_ref, meta_ref, place_ref, rank_hits_ref, row_hits_ref, scratch
    )


def grads_kernel(
    recv_ref,
    dims_ref,
    facts_ref,
    meta_ref,
    place_ref,
    rank_hits_ref,
    row_hits_ref,
    prob_half_ref,
    sums_half_ref,
    fact_ref,
    dim_ref,
    out_ref,
    prob_ref,
    *scratch,
):
    prob, sums = half(
        1, recv_ref, dims_ref, facts_ref, meta_ref, place_ref, rank_hits_ref, row_hits_ref, scratch
    )
    prob = prob + prob_half_ref[...]
    sums = sums + sums_half_ref[...]
    prob_ref[...] = prob
    residual = prob - places(place_ref)[1].astype(f32)
    grad_fact = jnp.sum(dot_nn(stacked_row(residual), fact_ref[...]), 0, keepdims=True)
    rows = jnp.concatenate([stacked_row(sums[i : i + 1]) for i in range(DIM_ROWS)], 1)
    side = DIM_ROWS // 2 * LANES
    both = dot_nn(
        jnp.concatenate([rows[:, :side], rows[:, side:]], 0),
        jnp.concatenate([dim_ref[:side, :], dim_ref[side:, :]], 1),
    )
    grad_dim = jnp.sum(both[:8, :LANES] + both[8:, LANES:], 0, keepdims=True)
    for owner in range(OWNERS):
        out_ref[owner, 0:1, :] = grad_fact
        out_ref[owner, 1:2, :] = grad_dim


def update_kernel(recv_ref, fact_weight_ref, dim_weight_ref, fact_out_ref, dim_out_ref):
    total = recv_ref[0]
    for peer in range(1, OWNERS):
        total = total + recv_ref[peer]
    scale = 0.5 / (OWNERS * FACTS_HERE) ** 0.5
    fact_out_ref[...] = fact_weight_ref[...] - scale * total[0:1]
    dim_out_ref[...] = dim_weight_ref[...] - scale * total[1:2]


HALF_SCRATCH = [
    pltpu.VMEM((CHIPS, LANES), f32),
    pltpu.VMEM((CHIPS, LANES), f32),
    pltpu.VMEM((CHIPS, LANES), jnp.int32),
    pltpu.VMEM((LANES, CHIPS * LANES), bf16),
    pltpu.VMEM((2 * DIM_ROWS, CHIPS * LANES), bf16),
]


def call(kernel, outs, scratch=(), in_specs=None, flops=None):
    extra = {} if in_specs is None else {"in_specs": in_specs}
    if flops is not None:
        extra["cost_estimate"] = pl.CostEstimate(
            flops=flops, bytes_accessed=1 << 20, transcendentals=0
        )
    return pl.pallas_call(
        kernel,
        name=kernel.__name__,
        out_shape=outs,
        scratch_shapes=list(scratch),
        compiler_params=pltpu.CompilerParams(vmem_limit_bytes=32 << 20),
        **extra,
    )


def exchange(value, axis, groups=None):
    return lax.all_to_all(
        value, axis, split_axis=0, concat_axis=0, tiled=True, axis_index_groups=groups
    )


def shards(fact_table, dim_table, fact_weight, dim_weight, bucket, row_index, labels):
    bucket = bucket.reshape(1, FACTS_HERE)
    row_index = row_index.reshape(1, FACTS_HERE)
    labels = labels.reshape(1, FACTS_HERE)
    fact_weight = fact_weight.reshape(1, LANES)
    dim_weight = dim_weight.reshape(1, LANES)
    core = (lax.axis_index("rows") & 1).reshape(1)
    in_hbm = pl.BlockSpec(memory_space=pltpu.HBM)

    def stay(array):
        return pltpu.with_memory_space_constraint(array, pltpu.HBM)

    (partial,) = call(
        scores_kernel,
        [pltpu.VMEM((PEERS, SCORE_ROWS, LANES), f32)],
        [
            pltpu.VMEM(fact_table.shape, bf16),
            pltpu.VMEM(dim_table.shape, bf16),
            pltpu.VMEM((2, LANES), f32),
            pltpu.SemaphoreType.DMA((2 + (len(fact_table) + len(dim_table)) // PIECE,)),
        ],
        [in_hbm] * 4,
    )(*[stay(array) for array in (fact_table, dim_table, fact_weight, dim_weight)])
    place, meta, rank_hits, row_hits = call(
        slots_kernel,
        [
            pltpu.VMEM((1, FACTS_HERE), jnp.int32),
            pltpu.VMEM((OWNERS, LANES), f32),
            pltpu.VMEM((LANES, FACTS_HERE), bf16),
            pltpu.VMEM((LANES, OWNERS * LANES), bf16),
        ],
        [pltpu.VMEM((3, FACTS_HERE), jnp.int32), pltpu.SemaphoreType.DMA((3,))],
        [pl.BlockSpec(memory_space=pltpu.SMEM)] + [in_hbm] * 3,
    )(core, *[stay(array) for array in (bucket, row_index, labels)])
    partial = exchange(partial, "feat")
    blocks, dims, facts = call(
        pack_kernel,
        [
            pltpu.VMEM((CHIPS, BLOCK_ROWS, LANES), f32),
            pltpu.VMEM((DIM_ROWS, LANES), f32),
            pltpu.VMEM((OWNERS, LANES), f32),
        ],
        [pltpu.VMEM((3 * OWNERS, FACTS_HERE), bf16)],
    )(partial, place, meta, rank_hits)
    blocks = exchange(
        blocks, "rows", [[2 * chip + core for chip in range(CHIPS)] for core in range(2)]
    )
    other_blocks = lax.ppermute(blocks, "rows", [(i, i ^ 1) for i in range(OWNERS)])
    prob_half, sums_half = call(
        same_core_kernel,
        [pltpu.VMEM((1, FACTS_HERE), f32), pltpu.VMEM((DIM_ROWS, LANES), f32)],
        HALF_SCRATCH,
        flops=1 << 31,
    )(blocks, dims, facts, meta, place, rank_hits, row_hits)
    grads, prob = call(
        grads_kernel,
        [
            pltpu.VMEM((OWNERS, 2, LANES), f32),
            jax.ShapeDtypeStruct((1, FACTS_HERE), f32),
        ],
        HALF_SCRATCH,
    )(
        other_blocks,
        dims,
        facts,
        meta,
        place,
        rank_hits,
        row_hits,
        prob_half,
        sums_half,
        fact_table,
        dim_table,
    )
    grads = exchange(grads, "rows")
    new_fact, new_dim = call(update_kernel, [jax.ShapeDtypeStruct((1, LANES), f32)] * 2)(
        grads, fact_weight, dim_weight
    )
    return new_fact.reshape(-1), new_dim.reshape(-1), prob.reshape(-1)


def solution(mesh):
    return jax.shard_map(
        shards,
        mesh=mesh,
        in_specs=(
            P("rows", "feat"),
            P("rows", "feat"),
            P("feat"),
            P("feat"),
            P("rows", None),
            P("rows"),
            P("rows"),
        ),
        out_specs=(P("feat"), P("feat"), P("rows")),
        check_vma=False,
    )
```

```python
import jax
import jax.numpy as jnp
from jax import lax
from jax.experimental import pallas as pl
from jax.experimental.pallas import tpu as pltpu
from jax.sharding import PartitionSpec as P

LANES = 128
OWNERS = 32
CHIPS = 16
PEERS = 8
DIM_ROWS = 32
FACT_ROWS = 16
FACTS_HERE = FACT_ROWS * LANES
SCORE_ROWS = DIM_ROWS + FACT_ROWS
BLOCK_ROWS = DIM_ROWS + 4
PIECE = 2048
LABEL_BIT = 12
VALID_BIT = 13

bf16 = jnp.bfloat16
f32 = jnp.float32


def split3(value):
    high = value.astype(bf16).astype(f32)
    rest = value - high
    middle = rest.astype(bf16).astype(f32)
    return high, middle, rest - middle


def stacked_row(row):
    shape = (8, row.shape[1])
    place = lax.broadcasted_iota(jnp.int32, shape, 0)
    high, middle, low = split3(row)
    return jnp.where(
        place == 0, high, jnp.where(place == 1, middle, jnp.where(place == 2, low, 0.0))
    ).astype(bf16)


def dot_nt(left, right):
    return lax.dot_general(
        left, right, (((1,), (1,)), ((), ())), preferred_element_type=f32
    )


def dot_nn(left, right):
    return jnp.dot(left, right, preferred_element_type=f32)


def hits(row, count):
    return lax.broadcasted_iota(jnp.int32, (count, row.shape[1]), 0) == row


def onehot(row, count):
    return jnp.where(hits(row, count), 1.0, 0.0).astype(bf16)


def place_facts(core, bucket, index, label, place_ref, meta_ref, rank_hits_ref):
    width = 2 * LANES
    chunks = FACTS_HERE // width
    upto = jnp.where(
        lax.broadcasted_iota(jnp.int32, (width, width), 0)
        <= lax.broadcasted_iota(jnp.int32, (width, width), 1),
        1.0,
        0.0,
    ).astype(bf16)
    owner = (bucket >> 1) + ((bucket & 1) ^ core) * CHIPS
    owner_hits = onehot(owner, OWNERS)
    stack = jnp.concatenate(
        [owner_hits[:, c * width : (c + 1) * width] for c in range(chunks)], 0
    )
    prefix = dot_nn(stack, upto)
    before = jnp.zeros((OWNERS, 1), f32)
    ranks = []
    for c in range(chunks):
        here = prefix[c * OWNERS : (c + 1) * OWNERS]
        mine = hits(owner[:, c * width : (c + 1) * width], OWNERS)
        ranks.append(jnp.sum(jnp.where(mine, here + before, 0.0), 0, keepdims=True))
        before = before + here[:, width - 1 : width]
    rank = jnp.concatenate(ranks, 1).astype(jnp.int32) - 1
    place_ref[...] = owner + (label << LABEL_BIT)
    low = (index & (LANES - 1)).astype(f32)
    high = ((index >> 7) + (label << (LABEL_BIT - 7)) + (1 << (VALID_BIT - 7))).astype(f32)
    mine = hits(owner, OWNERS)
    fields = jnp.concatenate([jnp.where(mine, low, 0.0), jnp.where(mine, high, 0.0)], 0)
    rank_hits = onehot(rank, LANES)
    rank_hits_ref[...] = rank_hits
    packed = dot_nt(fields.astype(bf16), rank_hits)
    meta_ref[...] = packed[:OWNERS] + packed[OWNERS:] * LANES


def prepare_kernel(
    core_ref,
    bucket_hbm,
    index_hbm,
    label_hbm,
    fact_hbm,
    dim_hbm,
    fact_weight_hbm,
    dim_weight_hbm,
    out_ref,
    place_ref,
    meta_ref,
    rank_hits_ref,
    given,
    weights,
    table,
    sems,
):
    loads = [
        pltpu.make_async_copy(source, given.at[pl.ds(i, 1)], sems.at[i])
        for i, source in enumerate((bucket_hbm, index_hbm, label_hbm))
    ] + [
        pltpu.make_async_copy(source, weights.at[pl.ds(i, 1)], sems.at[3 + i])
        for i, source in enumerate((fact_weight_hbm, dim_weight_hbm))
    ]
    pieces = []
    for first, source in ((0, dim_hbm), (dim_hbm.shape[0], fact_hbm)):
        for start in range(0, source.shape[0], PIECE):
            pieces.append(
                pltpu.make_async_copy(
                    source.at[pl.ds(start, PIECE)],
                    table.at[pl.ds(first + start, PIECE)],
                    sems.at[len(loads) + len(pieces)],
                )
            )
    for copy in loads + pieces:
        copy.start()
    for load in loads:
        load.wait()
    place_facts(
        core_ref[0],
        given[0:1, :],
        given[1:2, :],
        given[2:3, :],
        place_ref,
        meta_ref,
        rank_hits_ref,
    )
    terms = jnp.concatenate([stacked_row(weights[i : i + 1, :]) for i in range(2)], 0)
    for copy in pieces:
        copy.wait()
    parts = dot_nt(terms, table[...])
    for start, rows in ((8, range(DIM_ROWS)), (0, range(DIM_ROWS, SCORE_ROWS))):
        part = jnp.sum(
            parts[start : start + 8, rows[0] * LANES : (rows[-1] + 1) * LANES], 0, keepdims=True
        )
        for i, row in enumerate(rows):
            out_ref[0, row : row + 1, :] = part[:, i * LANES : (i + 1) * LANES]
    for peer in range(1, PEERS):
        out_ref[peer] = out_ref[0]


def places(place_ref):
    place = place_ref[...]
    return place & (OWNERS - 1), place >> LABEL_BIT


def pack_kernel(
    recv_ref, place_ref, meta_ref, rank_hits_ref, out_ref, dims_ref, facts_ref, left_ref
):
    total = recv_ref[0]
    for peer in range(1, PEERS):
        total = total + recv_ref[peer]
    dims_ref[...] = total[:DIM_ROWS]
    owner, _ = places(place_ref)
    for i in range(FACT_ROWS):
        cut = slice(i * LANES, (i + 1) * LANES)
        mine = hits(owner[:, cut], OWNERS)
        for part, value in enumerate(split3(total[DIM_ROWS + i : DIM_ROWS + i + 1])):
            left_ref[part * OWNERS : (part + 1) * OWNERS, cut] = jnp.where(mine, value, 0.0).astype(bf16)
    packed = dot_nt(left_ref[...], rank_hits_ref[...])
    packed = packed[:OWNERS] + packed[OWNERS : 2 * OWNERS] + packed[2 * OWNERS :]
    facts_ref[...] = packed
    for chip in range(CHIPS):
        out_ref[chip, :DIM_ROWS, :] = total[:DIM_ROWS]
        for other in range(2):
            row, slot = DIM_ROWS + other, other * CHIPS + chip
            out_ref[chip, row : row + 1, :] = packed[slot : slot + 1]
            out_ref[chip, row + 2 : row + 3, :] = meta_ref[slot : slot + 1, :]


def stacked(value, count=3):
    return jnp.concatenate(split3(value)[:count], 0).astype(bf16)


def summed(parts, count):
    total = parts[:count]
    for start in range(count, parts.shape[0], count):
        total = total + parts[start : start + count]
    return total


def taken(value, row):
    return jnp.sum(jnp.where(hits(row, value.shape[0]), value, 0.0), 0, keepdims=True)


def sigmoid(value):
    return 1.0 / (1.0 + jnp.exp(-value))


def half(
    other, recv_ref, dims_ref, facts_ref, meta_ref, place_ref, rank_hits_ref, row_hits_ref, scratch
):
    home_ref, own_ref, code_ref, low_ref, left_ref = scratch
    slots = slice(other * CHIPS, (other + 1) * CHIPS)
    meta = meta_ref[slots, :].astype(jnp.int32)
    dims = stacked(dims_ref[...])
    for chip in range(CHIPS):
        cut = slice(chip * LANES, (chip + 1) * LANES)
        parts = dot_nn(stacked(recv_ref[chip, :DIM_ROWS, :]), row_hits_ref[:, cut])
        home_ref[chip : chip + 1, :] = taken(
            summed(parts, DIM_ROWS), (meta[chip : chip + 1] >> 7) & (DIM_ROWS - 1)
        )
        row = DIM_ROWS + other
        code = recv_ref[chip, row + 2 : row + 3, :].astype(jnp.int32)
        code_ref[chip : chip + 1, :] = code
        column = onehot(code & (LANES - 1), LANES)
        low_ref[:, cut] = column
        own_ref[chip : chip + 1, :] = recv_ref[chip, row : row + 1, :] + taken(
            summed(dot_nn(dims, column), DIM_ROWS), (code >> 7) & (DIM_ROWS - 1)
        )
    prob = stacked(sigmoid(home_ref[...] + facts_ref[slots, :]), 2)
    prob = taken(
        summed(dot_nn(prob, rank_hits_ref[...]), CHIPS), places(place_ref)[0] - other * CHIPS
    )
    code = code_ref[...]
    residual = (sigmoid(own_ref[...]) - ((code >> LABEL_BIT) & 1).astype(f32)) * (
        code >> VALID_BIT
    ).astype(f32)
    terms = split3(residual)[:2]
    for chip in range(CHIPS):
        cut = slice(chip * LANES, (chip + 1) * LANES)
        mine = hits((code[chip : chip + 1] >> 7) & (DIM_ROWS - 1), DIM_ROWS)
        for part, value in enumerate(terms):
            left_ref[part * DIM_ROWS : (part + 1) * DIM_ROWS, cut] = jnp.where(
                mine, value[chip : chip + 1], 0.0
            ).astype(bf16)
    return prob, summed(dot_nt(left_ref[...], low_ref[...]), DIM_ROWS)


def same_core_kernel(
    recv_ref,
    dims_ref,
    facts_ref,
    meta_ref,
    place_ref,
    rank_hits_ref,
    prob_ref,
    sums_ref,
    row_hits_ref,
    here_ref,
    *scratch,
):
    meta = meta_ref[...].astype(jnp.int32) & (LANES - 1)
    for chip in range(CHIPS):
        cut = slice(chip * LANES, (chip + 1) * LANES)
        here_ref[:, cut] = onehot(meta[chip : chip + 1], LANES)
    prob_ref[...], sums_ref[...] = half(
        0, recv_ref, dims_ref, facts_ref, meta_ref, place_ref, rank_hits_ref, here_ref, scratch
    )
    for chip in range(CHIPS):
        cut = slice(chip * LANES, (chip + 1) * LANES)
        row_hits_ref[:, cut] = onehot(meta[CHIPS + chip : CHIPS + chip + 1], LANES)


def grads_kernel(
    recv_ref,
    dims_ref,
    facts_ref,
    meta_ref,
    place_ref,
    rank_hits_ref,
    row_hits_ref,
    prob_half_ref,
    sums_half_ref,
    fact_ref,
    dim_ref,
    out_ref,
    prob_ref,
    *scratch,
):
    prob, sums = half(
        1, recv_ref, dims_ref, facts_ref, meta_ref, place_ref, rank_hits_ref, row_hits_ref, scratch
    )
    prob = prob + prob_half_ref[...]
    sums = sums + sums_half_ref[...]
    prob_ref[...] = prob
    residual = prob - places(place_ref)[1].astype(f32)
    grad_fact = jnp.sum(dot_nn(stacked_row(residual), fact_ref[...]), 0, keepdims=True)
    rows = jnp.concatenate([stacked_row(sums[i : i + 1]) for i in range(DIM_ROWS)], 1)
    side = DIM_ROWS // 2 * LANES
    both = dot_nn(
        jnp.concatenate([rows[:, :side], rows[:, side:]], 0),
        jnp.concatenate([dim_ref[:side, :], dim_ref[side:, :]], 1),
    )
    grad_dim = jnp.sum(both[:8, :LANES] + both[8:, LANES:], 0, keepdims=True)
    for owner in range(OWNERS):
        out_ref[owner, 0:1, :] = grad_fact
        out_ref[owner, 1:2, :] = grad_dim


def update_kernel(recv_ref, fact_weight_ref, dim_weight_ref, fact_out_ref, dim_out_ref):
    total = recv_ref[0]
    for peer in range(1, OWNERS):
        total = total + recv_ref[peer]
    scale = 0.5 / (OWNERS * FACTS_HERE) ** 0.5
    fact_out_ref[...] = fact_weight_ref[...] - scale * total[0:1]
    dim_out_ref[...] = dim_weight_ref[...] - scale * total[1:2]


HALF_SCRATCH = [
    pltpu.VMEM((CHIPS, LANES), f32),
    pltpu.VMEM((CHIPS, LANES), f32),
    pltpu.VMEM((CHIPS, LANES), jnp.int32),
    pltpu.VMEM((LANES, CHIPS * LANES), bf16),
    pltpu.VMEM((2 * DIM_ROWS, CHIPS * LANES), bf16),
]


def call(kernel, outs, scratch=(), in_specs=None, flops=None):
    extra = {} if in_specs is None else {"in_specs": in_specs}
    if flops is not None:
        extra["cost_estimate"] = pl.CostEstimate(
            flops=flops, bytes_accessed=1 << 20, transcendentals=0
        )
    return pl.pallas_call(
        kernel,
        name=kernel.__name__,
        out_shape=outs,
        scratch_shapes=list(scratch),
        compiler_params=pltpu.CompilerParams(vmem_limit_bytes=32 << 20),
        **extra,
    )


def exchange(value, axis, groups=None):
    return lax.all_to_all(
        value, axis, split_axis=0, concat_axis=0, tiled=True, axis_index_groups=groups
    )


def shards(fact_table, dim_table, fact_weight, dim_weight, bucket, row_index, labels):
    bucket = bucket.reshape(1, FACTS_HERE)
    row_index = row_index.reshape(1, FACTS_HERE)
    labels = labels.reshape(1, FACTS_HERE)
    fact_weight = fact_weight.reshape(1, LANES)
    dim_weight = dim_weight.reshape(1, LANES)
    core = (lax.axis_index("rows") & 1).reshape(1)
    partial, place, meta, rank_hits = call(
        prepare_kernel,
        [
            pltpu.VMEM((PEERS, SCORE_ROWS, LANES), f32),
            pltpu.VMEM((1, FACTS_HERE), jnp.int32),
            pltpu.VMEM((OWNERS, LANES), f32),
            pltpu.VMEM((LANES, FACTS_HERE), bf16),
        ],
        [
            pltpu.VMEM((3, FACTS_HERE), jnp.int32),
            pltpu.VMEM((2, LANES), f32),
            pltpu.VMEM((SCORE_ROWS * LANES, LANES), bf16),
            pltpu.SemaphoreType.DMA((5 + (len(fact_table) + len(dim_table)) // PIECE,)),
        ],
        [pl.BlockSpec(memory_space=pltpu.SMEM)]
        + [pl.BlockSpec(memory_space=pltpu.HBM)] * 7,
    )(
        core,
        *[
            pltpu.with_memory_space_constraint(array, pltpu.HBM)
            for array in (
                bucket,
                row_index,
                labels,
                fact_table,
                dim_table,
                fact_weight,
                dim_weight,
            )
        ],
    )
    partial = exchange(partial, "feat")
    blocks, dims, facts = call(
        pack_kernel,
        [
            pltpu.VMEM((CHIPS, BLOCK_ROWS, LANES), f32),
            pltpu.VMEM((DIM_ROWS, LANES), f32),
            pltpu.VMEM((OWNERS, LANES), f32),
        ],
        [pltpu.VMEM((3 * OWNERS, FACTS_HERE), bf16)],
    )(partial, place, meta, rank_hits)
    blocks = exchange(
        blocks, "rows", [[2 * chip + core for chip in range(CHIPS)] for core in range(2)]
    )
    other_blocks = lax.ppermute(blocks, "rows", [(i, i ^ 1) for i in range(OWNERS)])
    prob_half, sums_half, row_hits = call(
        same_core_kernel,
        [
            pltpu.VMEM((1, FACTS_HERE), f32),
            pltpu.VMEM((DIM_ROWS, LANES), f32),
            pltpu.VMEM((LANES, CHIPS * LANES), bf16),
        ],
        [pltpu.VMEM((LANES, CHIPS * LANES), bf16)] + HALF_SCRATCH,
        flops=1 << 31,
    )(blocks, dims, facts, meta, place, rank_hits)
    grads, prob = call(
        grads_kernel,
        [
            pltpu.VMEM((OWNERS, 2, LANES), f32),
            jax.ShapeDtypeStruct((1, FACTS_HERE), f32),
        ],
        HALF_SCRATCH,
    )(
        other_blocks,
        dims,
        facts,
        meta,
        place,
        rank_hits,
        row_hits,
        prob_half,
        sums_half,
        fact_table,
        dim_table,
    )
    grads = exchange(grads, "rows")
    new_fact, new_dim = call(update_kernel, [jax.ShapeDtypeStruct((1, LANES), f32)] * 2)(
        grads, fact_weight, dim_weight
    )
    return new_fact.reshape(-1), new_dim.reshape(-1), prob.reshape(-1)


def solution(mesh):
    return jax.shard_map(
        shards,
        mesh=mesh,
        in_specs=(
            P("rows", "feat"),
            P("rows", "feat"),
            P("feat"),
            P("feat"),
            P("rows", None),
            P("rows"),
            P("rows"),
        ),
        out_specs=(P("feat"), P("feat"), P("rows")),
        check_vma=False,
    )
```

```python
import jax
import jax.numpy as jnp
from jax import lax
from jax.experimental import pallas as pl
from jax.experimental.pallas import tpu as pltpu
from jax.sharding import PartitionSpec as P

LANES = 128
OWNERS = 32
CHIPS = 16
PEERS = 8
DIM_ROWS = 32
FACT_ROWS = 16
FACTS_HERE = FACT_ROWS * LANES
SCORE_ROWS = DIM_ROWS + FACT_ROWS
BLOCK_ROWS = DIM_ROWS + 4
PIECE = 2048
LABEL_BIT = 12
VALID_BIT = 13

bf16 = jnp.bfloat16
f32 = jnp.float32


def split3(value):
    high = value.astype(bf16).astype(f32)
    rest = value - high
    middle = rest.astype(bf16).astype(f32)
    return high, middle, rest - middle


def stacked_row(row):
    shape = (8, row.shape[1])
    place = lax.broadcasted_iota(jnp.int32, shape, 0)
    high, middle, low = split3(row)
    return jnp.where(
        place == 0, high, jnp.where(place == 1, middle, jnp.where(place == 2, low, 0.0))
    ).astype(bf16)


def dot_nt(left, right):
    return lax.dot_general(
        left, right, (((1,), (1,)), ((), ())), preferred_element_type=f32
    )


def dot_nn(left, right):
    return jnp.dot(left, right, preferred_element_type=f32)


def hits(row, count):
    return lax.broadcasted_iota(jnp.int32, (count, row.shape[1]), 0) == row


def onehot(row, count):
    return jnp.where(hits(row, count), 1.0, 0.0).astype(bf16)


def side_of(row):
    return (row ^ (row >> 2)) & 1


def place_facts(side, bucket, index, label, place_ref, meta_ref, rank_hits_ref):
    width = 2 * LANES
    chunks = FACTS_HERE // width
    upto = jnp.where(
        lax.broadcasted_iota(jnp.int32, (width, width), 0)
        <= lax.broadcasted_iota(jnp.int32, (width, width), 1),
        1.0,
        0.0,
    ).astype(bf16)
    owner = (bucket >> 1) + (side_of(bucket) ^ side) * CHIPS
    owner_hits = onehot(owner, OWNERS)
    stack = jnp.concatenate(
        [owner_hits[:, c * width : (c + 1) * width] for c in range(chunks)], 0
    )
    prefix = dot_nn(stack, upto)
    before = jnp.zeros((OWNERS, 1), f32)
    ranks = []
    for c in range(chunks):
        here = prefix[c * OWNERS : (c + 1) * OWNERS]
        mine = hits(owner[:, c * width : (c + 1) * width], OWNERS)
        ranks.append(jnp.sum(jnp.where(mine, here + before, 0.0), 0, keepdims=True))
        before = before + here[:, width - 1 : width]
    rank = jnp.concatenate(ranks, 1).astype(jnp.int32) - 1
    place_ref[...] = owner + (label << LABEL_BIT)
    low = (index & (LANES - 1)).astype(f32)
    high = ((index >> 7) + (label << (LABEL_BIT - 7)) + (1 << (VALID_BIT - 7))).astype(f32)
    mine = hits(owner, OWNERS)
    fields = jnp.concatenate([jnp.where(mine, low, 0.0), jnp.where(mine, high, 0.0)], 0)
    rank_hits = onehot(rank, LANES)
    rank_hits_ref[...] = rank_hits
    packed = dot_nt(fields.astype(bf16), rank_hits)
    meta_ref[...] = packed[:OWNERS] + packed[OWNERS:] * LANES


def prepare_kernel(
    side_ref,
    bucket_hbm,
    index_hbm,
    label_hbm,
    fact_hbm,
    dim_hbm,
    fact_weight_hbm,
    dim_weight_hbm,
    out_ref,
    place_ref,
    meta_ref,
    rank_hits_ref,
    given,
    weights,
    table,
    sems,
):
    loads = [
        pltpu.make_async_copy(source, given.at[pl.ds(i, 1)], sems.at[i])
        for i, source in enumerate((bucket_hbm, index_hbm, label_hbm))
    ] + [
        pltpu.make_async_copy(source, weights.at[pl.ds(i, 1)], sems.at[3 + i])
        for i, source in enumerate((fact_weight_hbm, dim_weight_hbm))
    ]
    pieces = []
    for first, source in ((0, dim_hbm), (dim_hbm.shape[0], fact_hbm)):
        for start in range(0, source.shape[0], PIECE):
            pieces.append(
                pltpu.make_async_copy(
                    source.at[pl.ds(start, PIECE)],
                    table.at[pl.ds(first + start, PIECE)],
                    sems.at[len(loads) + len(pieces)],
                )
            )
    for copy in loads + pieces:
        copy.start()
    for load in loads:
        load.wait()
    place_facts(
        side_ref[0],
        given[0:1, :],
        given[1:2, :],
        given[2:3, :],
        place_ref,
        meta_ref,
        rank_hits_ref,
    )
    terms = jnp.concatenate([stacked_row(weights[i : i + 1, :]) for i in range(2)], 0)
    for copy in pieces:
        copy.wait()
    parts = dot_nt(terms, table[...])
    for start, rows in ((8, range(DIM_ROWS)), (0, range(DIM_ROWS, SCORE_ROWS))):
        part = jnp.sum(
            parts[start : start + 8, rows[0] * LANES : (rows[-1] + 1) * LANES], 0, keepdims=True
        )
        for i, row in enumerate(rows):
            out_ref[0, row : row + 1, :] = part[:, i * LANES : (i + 1) * LANES]
    for peer in range(1, PEERS):
        out_ref[peer] = out_ref[0]


def places(place_ref):
    place = place_ref[...]
    return place & (OWNERS - 1), place >> LABEL_BIT


def pack_kernel(
    recv_ref, place_ref, meta_ref, rank_hits_ref, out_ref, dims_ref, facts_ref, left_ref
):
    total = recv_ref[0]
    for peer in range(1, PEERS):
        total = total + recv_ref[peer]
    dims_ref[...] = total[:DIM_ROWS]
    owner, _ = places(place_ref)
    for i in range(FACT_ROWS):
        cut = slice(i * LANES, (i + 1) * LANES)
        mine = hits(owner[:, cut], OWNERS)
        for part, value in enumerate(split3(total[DIM_ROWS + i : DIM_ROWS + i + 1])):
            left_ref[part * OWNERS : (part + 1) * OWNERS, cut] = jnp.where(mine, value, 0.0).astype(bf16)
    packed = dot_nt(left_ref[...], rank_hits_ref[...])
    packed = packed[:OWNERS] + packed[OWNERS : 2 * OWNERS] + packed[2 * OWNERS :]
    facts_ref[...] = packed
    for chip in range(CHIPS):
        out_ref[chip, :DIM_ROWS, :] = total[:DIM_ROWS]
        for other in range(2):
            row, slot = DIM_ROWS + other, other * CHIPS + chip
            out_ref[chip, row : row + 1, :] = packed[slot : slot + 1]
            out_ref[chip, row + 2 : row + 3, :] = meta_ref[slot : slot + 1, :]


def stacked(value, count=3):
    return jnp.concatenate(split3(value)[:count], 0).astype(bf16)


def summed(parts, count):
    total = parts[:count]
    for start in range(count, parts.shape[0], count):
        total = total + parts[start : start + count]
    return total


def taken(value, row):
    return jnp.sum(jnp.where(hits(row, value.shape[0]), value, 0.0), 0, keepdims=True)


def sigmoid(value):
    return 1.0 / (1.0 + jnp.exp(-value))


def half(
    other, recv_ref, dims_ref, facts_ref, meta_ref, place_ref, rank_hits_ref, row_hits_ref, scratch
):
    home_ref, own_ref, code_ref, low_ref, left_ref = scratch
    slots = slice(other * CHIPS, (other + 1) * CHIPS)
    meta = meta_ref[slots, :].astype(jnp.int32)
    dims = stacked(dims_ref[...])
    for chip in range(CHIPS):
        cut = slice(chip * LANES, (chip + 1) * LANES)
        parts = dot_nn(stacked(recv_ref[chip, :DIM_ROWS, :]), row_hits_ref[:, cut])
        home_ref[chip : chip + 1, :] = taken(
            summed(parts, DIM_ROWS), (meta[chip : chip + 1] >> 7) & (DIM_ROWS - 1)
        )
        row = DIM_ROWS + other
        code = recv_ref[chip, row + 2 : row + 3, :].astype(jnp.int32)
        code_ref[:, cut] = code
        low_ref[:, cut] = onehot(code & (LANES - 1), LANES)
        own_ref[:, cut] = recv_ref[chip, row : row + 1, :]
    prob = stacked(sigmoid(home_ref[...] + facts_ref[slots, :]), 2)
    prob = taken(
        summed(dot_nn(prob, rank_hits_ref[...]), CHIPS), places(place_ref)[0] - other * CHIPS
    )
    code = code_ref[...]
    mine = hits((code >> 7) & (DIM_ROWS - 1), DIM_ROWS)
    score = summed(dot_nn(dims, low_ref[...]), DIM_ROWS)
    score = own_ref[...] + jnp.sum(jnp.where(mine, score, 0.0), 0, keepdims=True)
    residual = (sigmoid(score) - ((code >> LABEL_BIT) & 1).astype(f32)) * (
        code >> VALID_BIT
    ).astype(f32)
    for part, value in enumerate(split3(residual)[:2]):
        left_ref[part * DIM_ROWS : (part + 1) * DIM_ROWS, :] = jnp.where(mine, value, 0.0).astype(
            bf16
        )
    return prob, summed(dot_nt(left_ref[...], low_ref[...]), DIM_ROWS)


def same_side_kernel(
    recv_ref,
    dims_ref,
    facts_ref,
    meta_ref,
    place_ref,
    rank_hits_ref,
    prob_ref,
    sums_ref,
    row_hits_ref,
    here_ref,
    *scratch,
):
    meta = meta_ref[...].astype(jnp.int32) & (LANES - 1)
    for chip in range(CHIPS):
        cut = slice(chip * LANES, (chip + 1) * LANES)
        here_ref[:, cut] = onehot(meta[chip : chip + 1], LANES)
    prob_ref[...], sums_ref[...] = half(
        0, recv_ref, dims_ref, facts_ref, meta_ref, place_ref, rank_hits_ref, here_ref, scratch
    )
    for chip in range(CHIPS):
        cut = slice(chip * LANES, (chip + 1) * LANES)
        row_hits_ref[:, cut] = onehot(meta[CHIPS + chip : CHIPS + chip + 1], LANES)


def grads_kernel(
    recv_ref,
    dims_ref,
    facts_ref,
    meta_ref,
    place_ref,
    rank_hits_ref,
    row_hits_ref,
    prob_half_ref,
    sums_half_ref,
    fact_ref,
    dim_ref,
    out_ref,
    prob_ref,
    *scratch,
):
    prob, sums = half(
        1, recv_ref, dims_ref, facts_ref, meta_ref, place_ref, rank_hits_ref, row_hits_ref, scratch
    )
    prob = prob + prob_half_ref[...]
    sums = sums + sums_half_ref[...]
    prob_ref[...] = prob
    residual = prob - places(place_ref)[1].astype(f32)
    grad_fact = jnp.sum(dot_nn(stacked_row(residual), fact_ref[...]), 0, keepdims=True)
    rows = jnp.concatenate([stacked_row(sums[i : i + 1]) for i in range(DIM_ROWS)], 1)
    side = DIM_ROWS // 2 * LANES
    both = dot_nn(
        jnp.concatenate([rows[:, :side], rows[:, side:]], 0),
        jnp.concatenate([dim_ref[:side, :], dim_ref[side:, :]], 1),
    )
    grad_dim = jnp.sum(both[:8, :LANES] + both[8:, LANES:], 0, keepdims=True)
    for owner in range(OWNERS):
        out_ref[owner, 0:1, :] = grad_fact
        out_ref[owner, 1:2, :] = grad_dim


def update_kernel(recv_ref, fact_weight_ref, dim_weight_ref, fact_out_ref, dim_out_ref):
    total = recv_ref[0]
    for peer in range(1, OWNERS):
        total = total + recv_ref[peer]
    scale = 0.5 / (OWNERS * FACTS_HERE) ** 0.5
    fact_out_ref[...] = fact_weight_ref[...] - scale * total[0:1]
    dim_out_ref[...] = dim_weight_ref[...] - scale * total[1:2]


HALF_SCRATCH = [
    pltpu.VMEM((CHIPS, LANES), f32),
    pltpu.VMEM((1, CHIPS * LANES), f32),
    pltpu.VMEM((1, CHIPS * LANES), jnp.int32),
    pltpu.VMEM((LANES, CHIPS * LANES), bf16),
    pltpu.VMEM((2 * DIM_ROWS, CHIPS * LANES), bf16),
]


def call(kernel, outs, scratch=(), in_specs=None, flops=None):
    extra = {} if in_specs is None else {"in_specs": in_specs}
    if flops is not None:
        extra["cost_estimate"] = pl.CostEstimate(
            flops=flops, bytes_accessed=1 << 20, transcendentals=0
        )
    return pl.pallas_call(
        kernel,
        name=kernel.__name__,
        out_shape=outs,
        scratch_shapes=list(scratch),
        compiler_params=pltpu.CompilerParams(vmem_limit_bytes=32 << 20),
        **extra,
    )


def exchange(value, axis, groups=None):
    return lax.all_to_all(
        value, axis, split_axis=0, concat_axis=0, tiled=True, axis_index_groups=groups
    )


def shards(fact_table, dim_table, fact_weight, dim_weight, bucket, row_index, labels):
    bucket = bucket.reshape(1, FACTS_HERE)
    row_index = row_index.reshape(1, FACTS_HERE)
    labels = labels.reshape(1, FACTS_HERE)
    fact_weight = fact_weight.reshape(1, LANES)
    dim_weight = dim_weight.reshape(1, LANES)
    side = side_of(lax.axis_index("rows")).reshape(1)
    partial, place, meta, rank_hits = call(
        prepare_kernel,
        [
            pltpu.VMEM((PEERS, SCORE_ROWS, LANES), f32),
            pltpu.VMEM((1, FACTS_HERE), jnp.int32),
            pltpu.VMEM((OWNERS, LANES), f32),
            pltpu.VMEM((LANES, FACTS_HERE), bf16),
        ],
        [
            pltpu.VMEM((3, FACTS_HERE), jnp.int32),
            pltpu.VMEM((2, LANES), f32),
            pltpu.VMEM((SCORE_ROWS * LANES, LANES), bf16),
            pltpu.SemaphoreType.DMA((5 + (len(fact_table) + len(dim_table)) // PIECE,)),
        ],
        [pl.BlockSpec(memory_space=pltpu.SMEM)]
        + [pl.BlockSpec(memory_space=pltpu.HBM)] * 7,
    )(
        side,
        *[
            pltpu.with_memory_space_constraint(array, pltpu.HBM)
            for array in (
                bucket,
                row_index,
                labels,
                fact_table,
                dim_table,
                fact_weight,
                dim_weight,
            )
        ],
    )
    partial = exchange(partial, "feat")
    blocks, dims, facts = call(
        pack_kernel,
        [
            pltpu.VMEM((CHIPS, BLOCK_ROWS, LANES), f32),
            pltpu.VMEM((DIM_ROWS, LANES), f32),
            pltpu.VMEM((OWNERS, LANES), f32),
        ],
        [pltpu.VMEM((3 * OWNERS, FACTS_HERE), bf16)],
    )(partial, place, meta, rank_hits)
    blocks = exchange(
        blocks, "rows", [[i for i in range(OWNERS) if side_of(i) == side] for side in range(2)]
    )
    other_blocks = lax.ppermute(blocks, "rows", [(i, i ^ 1) for i in range(OWNERS)])
    prob_half, sums_half, row_hits = call(
        same_side_kernel,
        [
            pltpu.VMEM((1, FACTS_HERE), f32),
            pltpu.VMEM((DIM_ROWS, LANES), f32),
            pltpu.VMEM((LANES, CHIPS * LANES), bf16),
        ],
        [pltpu.VMEM((LANES, CHIPS * LANES), bf16)] + HALF_SCRATCH,
        flops=1 << 31,
    )(blocks, dims, facts, meta, place, rank_hits)
    grads, prob = call(
        grads_kernel,
        [
            pltpu.VMEM((OWNERS, 2, LANES), f32),
            jax.ShapeDtypeStruct((1, FACTS_HERE), f32),
        ],
        HALF_SCRATCH,
    )(
        other_blocks,
        dims,
        facts,
        meta,
        place,
        rank_hits,
        row_hits,
        prob_half,
        sums_half,
        fact_table,
        dim_table,
    )
    grads = exchange(grads, "rows")
    new_fact, new_dim = call(update_kernel, [jax.ShapeDtypeStruct((1, LANES), f32)] * 2)(
        grads, fact_weight, dim_weight
    )
    return new_fact.reshape(-1), new_dim.reshape(-1), prob.reshape(-1)


def solution(mesh):
    return jax.shard_map(
        shards,
        mesh=mesh,
        in_specs=(
            P("rows", "feat"),
            P("rows", "feat"),
            P("feat"),
            P("feat"),
            P("rows", None),
            P("rows"),
            P("rows"),
        ),
        out_specs=(P("feat"), P("feat"), P("rows")),
        check_vma=False,
    )
```

```python
import jax
import jax.numpy as jnp
from jax import lax
from jax.experimental import pallas as pl
from jax.experimental.pallas import tpu as pltpu
from jax.sharding import PartitionSpec as P

LANES = 128
OWNERS = 32
CHIPS = 16
PEERS = 8
DIM_ROWS = 32
FACT_ROWS = 16
FACTS_HERE = FACT_ROWS * LANES
SCORE_ROWS = DIM_ROWS + FACT_ROWS
BLOCK_ROWS = DIM_ROWS + 4
PIECE = 2048
LABEL_BIT = 12
VALID_BIT = 13

bf16 = jnp.bfloat16
f32 = jnp.float32


def split3(value):
    high = value.astype(bf16).astype(f32)
    rest = value - high
    middle = rest.astype(bf16).astype(f32)
    return high, middle, rest - middle


def stacked_row(row):
    shape = (8, row.shape[1])
    place = lax.broadcasted_iota(jnp.int32, shape, 0)
    high, middle, low = split3(row)
    return jnp.where(
        place == 0, high, jnp.where(place == 1, middle, jnp.where(place == 2, low, 0.0))
    ).astype(bf16)


def dot_nt(left, right):
    return lax.dot_general(
        left, right, (((1,), (1,)), ((), ())), preferred_element_type=f32
    )


def dot_nn(left, right):
    return jnp.dot(left, right, preferred_element_type=f32)


def hits(row, count):
    return lax.broadcasted_iota(jnp.int32, (count, row.shape[1]), 0) == row


def onehot(row, count):
    return jnp.where(hits(row, count), 1.0, 0.0).astype(bf16)


def side_of(row):
    return (row ^ (row >> 2)) & 1


def place_of(row):
    return (((row >> 1) & 3) << 2) + (row >> 3)


FEAT_ORDER = [7, 3, 5, 1, 6, 2, 4, 0]
SIDES = [
    sorted((row for row in range(OWNERS) if side_of(row) == side), key=place_of)
    for side in range(2)
]
CORE_ORDER = sorted(range(OWNERS), key=lambda row: row & 1)


def place_facts(side, bucket, index, label, place_ref, meta_ref, rank_hits_ref):
    width = 2 * LANES
    chunks = FACTS_HERE // width
    upto = jnp.where(
        lax.broadcasted_iota(jnp.int32, (width, width), 0)
        <= lax.broadcasted_iota(jnp.int32, (width, width), 1),
        1.0,
        0.0,
    ).astype(bf16)
    owner = place_of(bucket) + (side_of(bucket) ^ side) * CHIPS
    owner_hits = onehot(owner, OWNERS)
    stack = jnp.concatenate(
        [owner_hits[:, c * width : (c + 1) * width] for c in range(chunks)], 0
    )
    prefix = dot_nn(stack, upto)
    before = jnp.zeros((OWNERS, 1), f32)
    ranks = []
    for c in range(chunks):
        here = prefix[c * OWNERS : (c + 1) * OWNERS]
        mine = hits(owner[:, c * width : (c + 1) * width], OWNERS)
        ranks.append(jnp.sum(jnp.where(mine, here + before, 0.0), 0, keepdims=True))
        before = before + here[:, width - 1 : width]
    rank = jnp.concatenate(ranks, 1).astype(jnp.int32) - 1
    place_ref[...] = owner + (label << LABEL_BIT)
    low = (index & (LANES - 1)).astype(f32)
    high = ((index >> 7) + (label << (LABEL_BIT - 7)) + (1 << (VALID_BIT - 7))).astype(f32)
    mine = hits(owner, OWNERS)
    fields = jnp.concatenate([jnp.where(mine, low, 0.0), jnp.where(mine, high, 0.0)], 0)
    rank_hits = onehot(rank, LANES)
    rank_hits_ref[...] = rank_hits
    packed = dot_nt(fields.astype(bf16), rank_hits)
    meta_ref[...] = packed[:OWNERS] + packed[OWNERS:] * LANES


def prepare_kernel(
    side_ref,
    bucket_hbm,
    index_hbm,
    label_hbm,
    fact_hbm,
    dim_hbm,
    fact_weight_hbm,
    dim_weight_hbm,
    out_ref,
    place_ref,
    meta_ref,
    rank_hits_ref,
    given,
    weights,
    table,
    sems,
):
    loads = [
        pltpu.make_async_copy(source, given.at[pl.ds(i, 1)], sems.at[i])
        for i, source in enumerate((bucket_hbm, index_hbm, label_hbm))
    ] + [
        pltpu.make_async_copy(source, weights.at[pl.ds(i, 1)], sems.at[3 + i])
        for i, source in enumerate((fact_weight_hbm, dim_weight_hbm))
    ]
    pieces = []
    for first, source in ((0, dim_hbm), (dim_hbm.shape[0], fact_hbm)):
        for start in range(0, source.shape[0], PIECE):
            pieces.append(
                pltpu.make_async_copy(
                    source.at[pl.ds(start, PIECE)],
                    table.at[pl.ds(first + start, PIECE)],
                    sems.at[len(loads) + len(pieces)],
                )
            )
    for copy in loads + pieces:
        copy.start()
    for load in loads:
        load.wait()
    place_facts(
        side_ref[0],
        given[0:1, :],
        given[1:2, :],
        given[2:3, :],
        place_ref,
        meta_ref,
        rank_hits_ref,
    )
    terms = jnp.concatenate([stacked_row(weights[i : i + 1, :]) for i in range(2)], 0)
    for copy in pieces:
        copy.wait()
    parts = dot_nt(terms, table[...])
    for start, rows in ((8, range(DIM_ROWS)), (0, range(DIM_ROWS, SCORE_ROWS))):
        part = jnp.sum(
            parts[start : start + 8, rows[0] * LANES : (rows[-1] + 1) * LANES], 0, keepdims=True
        )
        for i, row in enumerate(rows):
            out_ref[0, row : row + 1, :] = part[:, i * LANES : (i + 1) * LANES]
    for peer in range(1, PEERS):
        out_ref[peer] = out_ref[0]


def places(place_ref):
    place = place_ref[...]
    return place & (OWNERS - 1), place >> LABEL_BIT


def pack_kernel(
    recv_ref, place_ref, meta_ref, rank_hits_ref, out_ref, dims_ref, facts_ref, left_ref
):
    total = recv_ref[0]
    for peer in range(1, PEERS):
        total = total + recv_ref[peer]
    dims_ref[...] = total[:DIM_ROWS]
    owner, _ = places(place_ref)
    for i in range(FACT_ROWS):
        cut = slice(i * LANES, (i + 1) * LANES)
        mine = hits(owner[:, cut], OWNERS)
        for part, value in enumerate(split3(total[DIM_ROWS + i : DIM_ROWS + i + 1])):
            left_ref[part * OWNERS : (part + 1) * OWNERS, cut] = jnp.where(mine, value, 0.0).astype(bf16)
    packed = dot_nt(left_ref[...], rank_hits_ref[...])
    packed = packed[:OWNERS] + packed[OWNERS : 2 * OWNERS] + packed[2 * OWNERS :]
    facts_ref[...] = packed
    for chip in range(CHIPS):
        out_ref[chip, :DIM_ROWS, :] = total[:DIM_ROWS]
        for other in range(2):
            row, slot = DIM_ROWS + other, other * CHIPS + chip
            out_ref[chip, row : row + 1, :] = packed[slot : slot + 1]
            out_ref[chip, row + 2 : row + 3, :] = meta_ref[slot : slot + 1, :]


def stacked(value, count=3):
    return jnp.concatenate(split3(value)[:count], 0).astype(bf16)


def summed(parts, count):
    total = parts[:count]
    for start in range(count, parts.shape[0], count):
        total = total + parts[start : start + count]
    return total


def taken(value, row):
    return jnp.sum(jnp.where(hits(row, value.shape[0]), value, 0.0), 0, keepdims=True)


def sigmoid(value):
    return 1.0 / (1.0 + jnp.exp(-value))


def half(
    other, recv_ref, dims_ref, facts_ref, meta_ref, place_ref, rank_hits_ref, row_hits_ref, scratch
):
    home_ref, own_ref, code_ref, low_ref, left_ref = scratch
    slots = slice(other * CHIPS, (other + 1) * CHIPS)
    meta = meta_ref[slots, :].astype(jnp.int32)
    dims = stacked(dims_ref[...])
    for chip in range(CHIPS):
        cut = slice(chip * LANES, (chip + 1) * LANES)
        parts = dot_nn(stacked(recv_ref[chip, :DIM_ROWS, :]), row_hits_ref[:, cut])
        home_ref[chip : chip + 1, :] = taken(
            summed(parts, DIM_ROWS), (meta[chip : chip + 1] >> 7) & (DIM_ROWS - 1)
        )
        row = DIM_ROWS + other
        code = recv_ref[chip, row + 2 : row + 3, :].astype(jnp.int32)
        code_ref[:, cut] = code
        low_ref[:, cut] = onehot(code & (LANES - 1), LANES)
        own_ref[:, cut] = recv_ref[chip, row : row + 1, :]
    prob = stacked(sigmoid(home_ref[...] + facts_ref[slots, :]), 2)
    prob = taken(
        summed(dot_nn(prob, rank_hits_ref[...]), CHIPS), places(place_ref)[0] - other * CHIPS
    )
    code = code_ref[...]
    mine = hits((code >> 7) & (DIM_ROWS - 1), DIM_ROWS)
    score = summed(dot_nn(dims, low_ref[...]), DIM_ROWS)
    score = own_ref[...] + jnp.sum(jnp.where(mine, score, 0.0), 0, keepdims=True)
    residual = (sigmoid(score) - ((code >> LABEL_BIT) & 1).astype(f32)) * (
        code >> VALID_BIT
    ).astype(f32)
    for part, value in enumerate(split3(residual)[:2]):
        left_ref[part * DIM_ROWS : (part + 1) * DIM_ROWS, :] = jnp.where(mine, value, 0.0).astype(
            bf16
        )
    return prob, summed(dot_nt(left_ref[...], low_ref[...]), DIM_ROWS)


def same_side_kernel(
    recv_ref,
    dims_ref,
    facts_ref,
    meta_ref,
    place_ref,
    rank_hits_ref,
    prob_ref,
    sums_ref,
    row_hits_ref,
    here_ref,
    *scratch,
):
    meta = meta_ref[...].astype(jnp.int32) & (LANES - 1)
    for chip in range(CHIPS):
        cut = slice(chip * LANES, (chip + 1) * LANES)
        here_ref[:, cut] = onehot(meta[chip : chip + 1], LANES)
    prob_ref[...], sums_ref[...] = half(
        0, recv_ref, dims_ref, facts_ref, meta_ref, place_ref, rank_hits_ref, here_ref, scratch
    )
    for chip in range(CHIPS):
        cut = slice(chip * LANES, (chip + 1) * LANES)
        row_hits_ref[:, cut] = onehot(meta[CHIPS + chip : CHIPS + chip + 1], LANES)


def grads_kernel(
    recv_ref,
    dims_ref,
    facts_ref,
    meta_ref,
    place_ref,
    rank_hits_ref,
    row_hits_ref,
    prob_half_ref,
    sums_half_ref,
    fact_ref,
    dim_ref,
    out_ref,
    prob_ref,
    *scratch,
):
    prob, sums = half(
        1, recv_ref, dims_ref, facts_ref, meta_ref, place_ref, rank_hits_ref, row_hits_ref, scratch
    )
    prob = prob + prob_half_ref[...]
    sums = sums + sums_half_ref[...]
    prob_ref[...] = prob
    residual = prob - places(place_ref)[1].astype(f32)
    grad_fact = jnp.sum(dot_nn(stacked_row(residual), fact_ref[...]), 0, keepdims=True)
    rows = jnp.concatenate([stacked_row(sums[i : i + 1]) for i in range(DIM_ROWS)], 1)
    side = DIM_ROWS // 2 * LANES
    both = dot_nn(
        jnp.concatenate([rows[:, :side], rows[:, side:]], 0),
        jnp.concatenate([dim_ref[:side, :], dim_ref[side:, :]], 1),
    )
    grad_dim = jnp.sum(both[:8, :LANES] + both[8:, LANES:], 0, keepdims=True)
    for owner in range(OWNERS):
        out_ref[owner, 0:1, :] = grad_fact
        out_ref[owner, 1:2, :] = grad_dim


def update_kernel(recv_ref, fact_weight_ref, dim_weight_ref, fact_out_ref, dim_out_ref):
    total = recv_ref[0]
    for peer in range(1, OWNERS):
        total = total + recv_ref[peer]
    scale = 0.5 / (OWNERS * FACTS_HERE) ** 0.5
    fact_out_ref[...] = fact_weight_ref[...] - scale * total[0:1]
    dim_out_ref[...] = dim_weight_ref[...] - scale * total[1:2]


HALF_SCRATCH = [
    pltpu.VMEM((CHIPS, LANES), f32),
    pltpu.VMEM((1, CHIPS * LANES), f32),
    pltpu.VMEM((1, CHIPS * LANES), jnp.int32),
    pltpu.VMEM((LANES, CHIPS * LANES), bf16),
    pltpu.VMEM((2 * DIM_ROWS, CHIPS * LANES), bf16),
]


def call(kernel, outs, scratch=(), in_specs=None, flops=None):
    extra = {} if in_specs is None else {"in_specs": in_specs}
    if flops is not None:
        extra["cost_estimate"] = pl.CostEstimate(
            flops=flops, bytes_accessed=1 << 20, transcendentals=0
        )
    return pl.pallas_call(
        kernel,
        name=kernel.__name__,
        out_shape=outs,
        scratch_shapes=list(scratch),
        compiler_params=pltpu.CompilerParams(vmem_limit_bytes=32 << 20),
        **extra,
    )


def exchange(value, axis, groups=None):
    return lax.all_to_all(
        value, axis, split_axis=0, concat_axis=0, tiled=True, axis_index_groups=groups
    )


def shards(fact_table, dim_table, fact_weight, dim_weight, bucket, row_index, labels):
    bucket = bucket.reshape(1, FACTS_HERE)
    row_index = row_index.reshape(1, FACTS_HERE)
    labels = labels.reshape(1, FACTS_HERE)
    fact_weight = fact_weight.reshape(1, LANES)
    dim_weight = dim_weight.reshape(1, LANES)
    side = side_of(lax.axis_index("rows")).reshape(1)
    partial, place, meta, rank_hits = call(
        prepare_kernel,
        [
            pltpu.VMEM((PEERS, SCORE_ROWS, LANES), f32),
            pltpu.VMEM((1, FACTS_HERE), jnp.int32),
            pltpu.VMEM((OWNERS, LANES), f32),
            pltpu.VMEM((LANES, FACTS_HERE), bf16),
        ],
        [
            pltpu.VMEM((3, FACTS_HERE), jnp.int32),
            pltpu.VMEM((2, LANES), f32),
            pltpu.VMEM((SCORE_ROWS * LANES, LANES), bf16),
            pltpu.SemaphoreType.DMA((5 + (len(fact_table) + len(dim_table)) // PIECE,)),
        ],
        [pl.BlockSpec(memory_space=pltpu.SMEM)]
        + [pl.BlockSpec(memory_space=pltpu.HBM)] * 7,
    )(
        side,
        *[
            pltpu.with_memory_space_constraint(array, pltpu.HBM)
            for array in (
                bucket,
                row_index,
                labels,
                fact_table,
                dim_table,
                fact_weight,
                dim_weight,
            )
        ],
    )
    partial = exchange(partial, "feat", [FEAT_ORDER])
    blocks, dims, facts = call(
        pack_kernel,
        [
            pltpu.VMEM((CHIPS, BLOCK_ROWS, LANES), f32),
            pltpu.VMEM((DIM_ROWS, LANES), f32),
            pltpu.VMEM((OWNERS, LANES), f32),
        ],
        [pltpu.VMEM((3 * OWNERS, FACTS_HERE), bf16)],
    )(partial, place, meta, rank_hits)
    blocks = exchange(
        blocks, "rows", SIDES
    )
    other_blocks = lax.ppermute(blocks, "rows", [(i, i ^ 1) for i in range(OWNERS)])
    prob_half, sums_half, row_hits = call(
        same_side_kernel,
        [
            pltpu.VMEM((1, FACTS_HERE), f32),
            pltpu.VMEM((DIM_ROWS, LANES), f32),
            pltpu.VMEM((LANES, CHIPS * LANES), bf16),
        ],
        [pltpu.VMEM((LANES, CHIPS * LANES), bf16)] + HALF_SCRATCH,
        flops=1 << 31,
    )(blocks, dims, facts, meta, place, rank_hits)
    grads, prob = call(
        grads_kernel,
        [
            pltpu.VMEM((OWNERS, 2, LANES), f32),
            jax.ShapeDtypeStruct((1, FACTS_HERE), f32),
        ],
        HALF_SCRATCH,
    )(
        other_blocks,
        dims,
        facts,
        meta,
        place,
        rank_hits,
        row_hits,
        prob_half,
        sums_half,
        fact_table,
        dim_table,
    )
    grads = exchange(grads, "rows", [CORE_ORDER])
    new_fact, new_dim = call(update_kernel, [jax.ShapeDtypeStruct((1, LANES), f32)] * 2)(
        grads, fact_weight, dim_weight
    )
    return new_fact.reshape(-1), new_dim.reshape(-1), prob.reshape(-1)


def solution(mesh):
    return jax.shard_map(
        shards,
        mesh=mesh,
        in_specs=(
            P("rows", "feat"),
            P("rows", "feat"),
            P("feat"),
            P("feat"),
            P("rows", None),
            P("rows"),
            P("rows"),
        ),
        out_specs=(P("feat"), P("feat"), P("rows")),
        check_vma=False,
    )
```

```python
import jax
import jax.numpy as jnp
from jax import lax
from jax.experimental import pallas as pl
from jax.experimental.pallas import tpu as pltpu
from jax.sharding import PartitionSpec as P

LANES = 128
OWNERS = 32
CHIPS = 16
PEERS = 8
DIM_ROWS = 32
FACT_ROWS = 16
FACTS_HERE = FACT_ROWS * LANES
SCORE_ROWS = DIM_ROWS + FACT_ROWS
BLOCK_ROWS = DIM_ROWS + 4
PIECE = 2048
LABEL_BIT = 12
VALID_BIT = 13

bf16 = jnp.bfloat16
f32 = jnp.float32


def split3(value):
    high = value.astype(bf16).astype(f32)
    rest = value - high
    middle = rest.astype(bf16).astype(f32)
    return high, middle, rest - middle


def stacked_row(row):
    shape = (8, row.shape[1])
    place = lax.broadcasted_iota(jnp.int32, shape, 0)
    high, middle, low = split3(row)
    return jnp.where(
        place == 0, high, jnp.where(place == 1, middle, jnp.where(place == 2, low, 0.0))
    ).astype(bf16)


def dot_nt(left, right):
    return lax.dot_general(
        left, right, (((1,), (1,)), ((), ())), preferred_element_type=f32
    )


def dot_nn(left, right):
    return jnp.dot(left, right, preferred_element_type=f32)


def hits(row, count):
    return lax.broadcasted_iota(jnp.int32, (count, row.shape[1]), 0) == row


def onehot(row, count):
    return jnp.where(hits(row, count), 1.0, 0.0).astype(bf16)


def side_of(row):
    return (row ^ (row >> 2)) & 1


def place_of(row):
    return CHIPS - 1 - (((row >> 1) & 3) << 2) - (row >> 3)


FEAT_ORDER = [7, 3, 6, 2, 5, 1, 4, 0]
SIDES = [
    sorted((row for row in range(OWNERS) if side_of(row) == side), key=place_of)
    for side in range(2)
]
ROW_ORDER = list(range(OWNERS))[::-1]


def place_facts(side, bucket, index, label, place_ref, meta_ref, rank_hits_ref):
    width = 2 * LANES
    chunks = FACTS_HERE // width
    upto = jnp.where(
        lax.broadcasted_iota(jnp.int32, (width, width), 0)
        <= lax.broadcasted_iota(jnp.int32, (width, width), 1),
        1.0,
        0.0,
    ).astype(bf16)
    owner = place_of(bucket) + (side_of(bucket) ^ side) * CHIPS
    owner_hits = onehot(owner, OWNERS)
    stack = jnp.concatenate(
        [owner_hits[:, c * width : (c + 1) * width] for c in range(chunks)], 0
    )
    prefix = dot_nn(stack, upto)
    before = jnp.zeros((OWNERS, 1), f32)
    ranks = []
    for c in range(chunks):
        here = prefix[c * OWNERS : (c + 1) * OWNERS]
        mine = hits(owner[:, c * width : (c + 1) * width], OWNERS)
        ranks.append(jnp.sum(jnp.where(mine, here + before, 0.0), 0, keepdims=True))
        before = before + here[:, width - 1 : width]
    rank = jnp.concatenate(ranks, 1).astype(jnp.int32) - 1
    place_ref[...] = owner + (label << LABEL_BIT)
    low = (index & (LANES - 1)).astype(f32)
    high = ((index >> 7) + (label << (LABEL_BIT - 7)) + (1 << (VALID_BIT - 7))).astype(f32)
    mine = hits(owner, OWNERS)
    fields = jnp.concatenate([jnp.where(mine, low, 0.0), jnp.where(mine, high, 0.0)], 0)
    rank_hits = onehot(rank, LANES)
    rank_hits_ref[...] = rank_hits
    packed = dot_nt(fields.astype(bf16), rank_hits)
    meta_ref[...] = packed[:OWNERS] + packed[OWNERS:] * LANES


def prepare_kernel(
    side_ref,
    bucket_hbm,
    index_hbm,
    label_hbm,
    fact_hbm,
    dim_hbm,
    fact_weight_hbm,
    dim_weight_hbm,
    out_ref,
    place_ref,
    meta_ref,
    rank_hits_ref,
    given,
    weights,
    table,
    sems,
):
    loads = [
        pltpu.make_async_copy(source, given.at[pl.ds(i, 1)], sems.at[i])
        for i, source in enumerate((bucket_hbm, index_hbm, label_hbm))
    ] + [
        pltpu.make_async_copy(source, weights.at[pl.ds(i, 1)], sems.at[3 + i])
        for i, source in enumerate((fact_weight_hbm, dim_weight_hbm))
    ]
    pieces = []
    for first, source in ((0, dim_hbm), (dim_hbm.shape[0], fact_hbm)):
        for start in range(0, source.shape[0], PIECE):
            pieces.append(
                pltpu.make_async_copy(
                    source.at[pl.ds(start, PIECE)],
                    table.at[pl.ds(first + start, PIECE)],
                    sems.at[len(loads) + len(pieces)],
                )
            )
    for copy in loads + pieces:
        copy.start()
    for load in loads:
        load.wait()
    place_facts(
        side_ref[0],
        given[0:1, :],
        given[1:2, :],
        given[2:3, :],
        place_ref,
        meta_ref,
        rank_hits_ref,
    )
    terms = jnp.concatenate([stacked_row(weights[i : i + 1, :]) for i in range(2)], 0)
    for copy in pieces:
        copy.wait()
    parts = dot_nt(terms, table[...])
    for start, rows in ((8, range(DIM_ROWS)), (0, range(DIM_ROWS, SCORE_ROWS))):
        part = jnp.sum(
            parts[start : start + 8, rows[0] * LANES : (rows[-1] + 1) * LANES], 0, keepdims=True
        )
        for i, row in enumerate(rows):
            out_ref[0, row : row + 1, :] = part[:, i * LANES : (i + 1) * LANES]
    for peer in range(1, PEERS):
        out_ref[peer] = out_ref[0]


def places(place_ref):
    place = place_ref[...]
    return place & (OWNERS - 1), place >> LABEL_BIT


def pack_kernel(
    recv_ref, place_ref, meta_ref, rank_hits_ref, out_ref, dims_ref, facts_ref, left_ref
):
    total = recv_ref[0]
    for peer in range(1, PEERS):
        total = total + recv_ref[peer]
    dims_ref[...] = total[:DIM_ROWS]
    owner, _ = places(place_ref)
    for i in range(FACT_ROWS):
        cut = slice(i * LANES, (i + 1) * LANES)
        mine = hits(owner[:, cut], OWNERS)
        for part, value in enumerate(split3(total[DIM_ROWS + i : DIM_ROWS + i + 1])):
            left_ref[part * OWNERS : (part + 1) * OWNERS, cut] = jnp.where(mine, value, 0.0).astype(bf16)
    packed = dot_nt(left_ref[...], rank_hits_ref[...])
    packed = packed[:OWNERS] + packed[OWNERS : 2 * OWNERS] + packed[2 * OWNERS :]
    facts_ref[...] = packed
    for chip in range(CHIPS):
        out_ref[chip, :DIM_ROWS, :] = total[:DIM_ROWS]
        for other in range(2):
            row, slot = DIM_ROWS + other, other * CHIPS + chip
            out_ref[chip, row : row + 1, :] = packed[slot : slot + 1]
            out_ref[chip, row + 2 : row + 3, :] = meta_ref[slot : slot + 1, :]


def stacked(value, count=3):
    return jnp.concatenate(split3(value)[:count], 0).astype(bf16)


def summed(parts, count):
    total = parts[:count]
    for start in range(count, parts.shape[0], count):
        total = total + parts[start : start + count]
    return total


def taken(value, row):
    return jnp.sum(jnp.where(hits(row, value.shape[0]), value, 0.0), 0, keepdims=True)


def sigmoid(value):
    return 1.0 / (1.0 + jnp.exp(-value))


def half(
    other, recv_ref, dims_ref, facts_ref, meta_ref, place_ref, rank_hits_ref, row_hits_ref, scratch
):
    home_ref, own_ref, code_ref, low_ref, left_ref = scratch
    slots = slice(other * CHIPS, (other + 1) * CHIPS)
    meta = meta_ref[slots, :].astype(jnp.int32)
    dims = stacked(dims_ref[...])
    for chip in range(CHIPS):
        cut = slice(chip * LANES, (chip + 1) * LANES)
        parts = dot_nn(stacked(recv_ref[chip, :DIM_ROWS, :]), row_hits_ref[:, cut])
        home_ref[chip : chip + 1, :] = taken(
            summed(parts, DIM_ROWS), (meta[chip : chip + 1] >> 7) & (DIM_ROWS - 1)
        )
        row = DIM_ROWS + other
        code = recv_ref[chip, row + 2 : row + 3, :].astype(jnp.int32)
        code_ref[:, cut] = code
        low_ref[:, cut] = onehot(code & (LANES - 1), LANES)
        own_ref[:, cut] = recv_ref[chip, row : row + 1, :]
    prob = stacked(sigmoid(home_ref[...] + facts_ref[slots, :]), 2)
    prob = taken(
        summed(dot_nn(prob, rank_hits_ref[...]), CHIPS), places(place_ref)[0] - other * CHIPS
    )
    code = code_ref[...]
    mine = hits((code >> 7) & (DIM_ROWS - 1), DIM_ROWS)
    score = summed(dot_nn(dims, low_ref[...]), DIM_ROWS)
    score = own_ref[...] + jnp.sum(jnp.where(mine, score, 0.0), 0, keepdims=True)
    residual = (sigmoid(score) - ((code >> LABEL_BIT) & 1).astype(f32)) * (
        code >> VALID_BIT
    ).astype(f32)
    for part, value in enumerate(split3(residual)[:2]):
        left_ref[part * DIM_ROWS : (part + 1) * DIM_ROWS, :] = jnp.where(mine, value, 0.0).astype(
            bf16
        )
    return prob, summed(dot_nt(left_ref[...], low_ref[...]), DIM_ROWS)


def same_side_kernel(
    recv_ref,
    dims_ref,
    facts_ref,
    meta_ref,
    place_ref,
    rank_hits_ref,
    prob_ref,
    sums_ref,
    row_hits_ref,
    here_ref,
    *scratch,
):
    meta = meta_ref[...].astype(jnp.int32) & (LANES - 1)
    for chip in range(CHIPS):
        cut = slice(chip * LANES, (chip + 1) * LANES)
        here_ref[:, cut] = onehot(meta[chip : chip + 1], LANES)
    prob_ref[...], sums_ref[...] = half(
        0, recv_ref, dims_ref, facts_ref, meta_ref, place_ref, rank_hits_ref, here_ref, scratch
    )
    for chip in range(CHIPS):
        cut = slice(chip * LANES, (chip + 1) * LANES)
        row_hits_ref[:, cut] = onehot(meta[CHIPS + chip : CHIPS + chip + 1], LANES)


def grads_kernel(
    recv_ref,
    dims_ref,
    facts_ref,
    meta_ref,
    place_ref,
    rank_hits_ref,
    row_hits_ref,
    prob_half_ref,
    sums_half_ref,
    fact_ref,
    dim_ref,
    out_ref,
    prob_ref,
    *scratch,
):
    prob, sums = half(
        1, recv_ref, dims_ref, facts_ref, meta_ref, place_ref, rank_hits_ref, row_hits_ref, scratch
    )
    prob = prob + prob_half_ref[...]
    sums = sums + sums_half_ref[...]
    prob_ref[...] = prob
    residual = prob - places(place_ref)[1].astype(f32)
    grad_fact = jnp.sum(dot_nn(stacked_row(residual), fact_ref[...]), 0, keepdims=True)
    rows = jnp.concatenate([stacked_row(sums[i : i + 1]) for i in range(DIM_ROWS)], 1)
    side = DIM_ROWS // 2 * LANES
    both = dot_nn(
        jnp.concatenate([rows[:, :side], rows[:, side:]], 0),
        jnp.concatenate([dim_ref[:side, :], dim_ref[side:, :]], 1),
    )
    grad_dim = jnp.sum(both[:8, :LANES] + both[8:, LANES:], 0, keepdims=True)
    for owner in range(OWNERS):
        out_ref[owner, 0:1, :] = grad_fact
        out_ref[owner, 1:2, :] = grad_dim


def update_kernel(recv_ref, fact_weight_ref, dim_weight_ref, fact_out_ref, dim_out_ref):
    total = recv_ref[0]
    for peer in range(1, OWNERS):
        total = total + recv_ref[peer]
    scale = 0.5 / (OWNERS * FACTS_HERE) ** 0.5
    fact_out_ref[...] = fact_weight_ref[...] - scale * total[0:1]
    dim_out_ref[...] = dim_weight_ref[...] - scale * total[1:2]


HALF_SCRATCH = [
    pltpu.VMEM((CHIPS, LANES), f32),
    pltpu.VMEM((1, CHIPS * LANES), f32),
    pltpu.VMEM((1, CHIPS * LANES), jnp.int32),
    pltpu.VMEM((LANES, CHIPS * LANES), bf16),
    pltpu.VMEM((2 * DIM_ROWS, CHIPS * LANES), bf16),
]


def call(kernel, outs, scratch=(), in_specs=None, flops=None):
    extra = {} if in_specs is None else {"in_specs": in_specs}
    if flops is not None:
        extra["cost_estimate"] = pl.CostEstimate(
            flops=flops, bytes_accessed=1 << 20, transcendentals=0
        )
    return pl.pallas_call(
        kernel,
        name=kernel.__name__,
        out_shape=outs,
        scratch_shapes=list(scratch),
        compiler_params=pltpu.CompilerParams(vmem_limit_bytes=32 << 20),
        **extra,
    )


def exchange(value, axis, groups=None):
    return lax.all_to_all(
        value, axis, split_axis=0, concat_axis=0, tiled=True, axis_index_groups=groups
    )


def shards(fact_table, dim_table, fact_weight, dim_weight, bucket, row_index, labels):
    bucket = bucket.reshape(1, FACTS_HERE)
    row_index = row_index.reshape(1, FACTS_HERE)
    labels = labels.reshape(1, FACTS_HERE)
    fact_weight = fact_weight.reshape(1, LANES)
    dim_weight = dim_weight.reshape(1, LANES)
    side = side_of(lax.axis_index("rows")).reshape(1)
    partial, place, meta, rank_hits = call(
        prepare_kernel,
        [
            pltpu.VMEM((PEERS, SCORE_ROWS, LANES), f32),
            pltpu.VMEM((1, FACTS_HERE), jnp.int32),
            pltpu.VMEM((OWNERS, LANES), f32),
            pltpu.VMEM((LANES, FACTS_HERE), bf16),
        ],
        [
            pltpu.VMEM((3, FACTS_HERE), jnp.int32),
            pltpu.VMEM((2, LANES), f32),
            pltpu.VMEM((SCORE_ROWS * LANES, LANES), bf16),
            pltpu.SemaphoreType.DMA((5 + (len(fact_table) + len(dim_table)) // PIECE,)),
        ],
        [pl.BlockSpec(memory_space=pltpu.SMEM)]
        + [pl.BlockSpec(memory_space=pltpu.HBM)] * 7,
    )(
        side,
        *[
            pltpu.with_memory_space_constraint(array, pltpu.HBM)
            for array in (
                bucket,
                row_index,
                labels,
                fact_table,
                dim_table,
                fact_weight,
                dim_weight,
            )
        ],
    )
    partial = exchange(partial, "feat", [FEAT_ORDER])
    blocks, dims, facts = call(
        pack_kernel,
        [
            pltpu.VMEM((CHIPS, BLOCK_ROWS, LANES), f32),
            pltpu.VMEM((DIM_ROWS, LANES), f32),
            pltpu.VMEM((OWNERS, LANES), f32),
        ],
        [pltpu.VMEM((3 * OWNERS, FACTS_HERE), bf16)],
    )(partial, place, meta, rank_hits)
    blocks = exchange(
        blocks, "rows", SIDES
    )
    other_blocks = lax.ppermute(blocks, "rows", [(i, i ^ 1) for i in range(OWNERS)])
    prob_half, sums_half, row_hits = call(
        same_side_kernel,
        [
            pltpu.VMEM((1, FACTS_HERE), f32),
            pltpu.VMEM((DIM_ROWS, LANES), f32),
            pltpu.VMEM((LANES, CHIPS * LANES), bf16),
        ],
        [pltpu.VMEM((LANES, CHIPS * LANES), bf16)] + HALF_SCRATCH,
        flops=1 << 31,
    )(blocks, dims, facts, meta, place, rank_hits)
    grads, prob = call(
        grads_kernel,
        [
            pltpu.VMEM((OWNERS, 2, LANES), f32),
            jax.ShapeDtypeStruct((1, FACTS_HERE), f32),
        ],
        HALF_SCRATCH,
    )(
        other_blocks,
        dims,
        facts,
        meta,
        place,
        rank_hits,
        row_hits,
        prob_half,
        sums_half,
        fact_table,
        dim_table,
    )
    grads = exchange(grads, "rows", [ROW_ORDER])
    new_fact, new_dim = call(update_kernel, [jax.ShapeDtypeStruct((1, LANES), f32)] * 2)(
        grads, fact_weight, dim_weight
    )
    return new_fact.reshape(-1), new_dim.reshape(-1), prob.reshape(-1)


def solution(mesh):
    return jax.shard_map(
        shards,
        mesh=mesh,
        in_specs=(
            P("rows", "feat"),
            P("rows", "feat"),
            P("feat"),
            P("feat"),
            P("rows", None),
            P("rows"),
            P("rows"),
        ),
        out_specs=(P("feat"), P("feat"), P("rows")),
        check_vma=False,
    )
```

```python
import jax
import jax.numpy as jnp
from jax import lax
from jax.experimental import pallas as pl
from jax.experimental.pallas import tpu as pltpu
from jax.sharding import PartitionSpec as P

LANES = 128
OWNERS = 32
CHIPS = 16
PEERS = 8
DIM_ROWS = 32
FACT_ROWS = 16
FACTS_HERE = FACT_ROWS * LANES
SCORE_ROWS = DIM_ROWS + FACT_ROWS
BLOCK_ROWS = DIM_ROWS + 4
PIECE = 2048
LABEL_BIT = 12
VALID_BIT = 13

bf16 = jnp.bfloat16
f32 = jnp.float32


def split3(value):
    high = value.astype(bf16).astype(f32)
    rest = value - high
    middle = rest.astype(bf16).astype(f32)
    return high, middle, rest - middle


def stacked_row(row):
    shape = (8, row.shape[1])
    place = lax.broadcasted_iota(jnp.int32, shape, 0)
    high, middle, low = split3(row)
    return jnp.where(
        place == 0, high, jnp.where(place == 1, middle, jnp.where(place == 2, low, 0.0))
    ).astype(bf16)


def dot_nt(left, right):
    return lax.dot_general(
        left, right, (((1,), (1,)), ((), ())), preferred_element_type=f32
    )


def dot_nn(left, right):
    return jnp.dot(left, right, preferred_element_type=f32)


def hits(row, count):
    return lax.broadcasted_iota(jnp.int32, (count, row.shape[1]), 0) == row


def onehot(row, count):
    return jnp.where(hits(row, count), 1.0, 0.0).astype(bf16)


def side_of(row):
    return (row ^ (row >> 2)) & 1


def place_of(row):
    return CHIPS - 1 - (((row >> 1) & 3) << 2) - (row >> 3)


FEAT_ORDER = [7, 3, 6, 2, 5, 1, 4, 0]
SIDES = [
    sorted((row for row in range(OWNERS) if side_of(row) == side), key=place_of)
    for side in range(2)
]
FAR = [0, 1, 3, 2]
ROW_ORDER = sorted(
    range(OWNERS), key=lambda row: (-FAR[row >> 3] - FAR[(row >> 1) & 3], -row)
)


def place_facts(side, bucket, index, label, place_ref, meta_ref, rank_hits_ref):
    width = 2 * LANES
    chunks = FACTS_HERE // width
    upto = jnp.where(
        lax.broadcasted_iota(jnp.int32, (width, width), 0)
        <= lax.broadcasted_iota(jnp.int32, (width, width), 1),
        1.0,
        0.0,
    ).astype(bf16)
    owner = place_of(bucket) + (side_of(bucket) ^ side) * CHIPS
    owner_hits = onehot(owner, OWNERS)
    stack = jnp.concatenate(
        [owner_hits[:, c * width : (c + 1) * width] for c in range(chunks)], 0
    )
    prefix = dot_nn(stack, upto)
    before = jnp.zeros((OWNERS, 1), f32)
    ranks = []
    for c in range(chunks):
        here = prefix[c * OWNERS : (c + 1) * OWNERS]
        mine = hits(owner[:, c * width : (c + 1) * width], OWNERS)
        ranks.append(jnp.sum(jnp.where(mine, here + before, 0.0), 0, keepdims=True))
        before = before + here[:, width - 1 : width]
    rank = jnp.concatenate(ranks, 1).astype(jnp.int32) - 1
    place_ref[...] = owner + (label << LABEL_BIT)
    low = (index & (LANES - 1)).astype(f32)
    high = ((index >> 7) + (label << (LABEL_BIT - 7)) + (1 << (VALID_BIT - 7))).astype(f32)
    mine = hits(owner, OWNERS)
    fields = jnp.concatenate([jnp.where(mine, low, 0.0), jnp.where(mine, high, 0.0)], 0)
    rank_hits = onehot(rank, LANES)
    rank_hits_ref[...] = rank_hits
    packed = dot_nt(fields.astype(bf16), rank_hits)
    meta_ref[...] = packed[:OWNERS] + packed[OWNERS:] * LANES


def prepare_kernel(
    side_ref,
    bucket_hbm,
    index_hbm,
    label_hbm,
    fact_hbm,
    dim_hbm,
    fact_weight_hbm,
    dim_weight_hbm,
    out_ref,
    place_ref,
    meta_ref,
    rank_hits_ref,
    given,
    weights,
    table,
    sems,
):
    loads = [
        pltpu.make_async_copy(source, given.at[pl.ds(i, 1)], sems.at[i])
        for i, source in enumerate((bucket_hbm, index_hbm, label_hbm))
    ] + [
        pltpu.make_async_copy(source, weights.at[pl.ds(i, 1)], sems.at[3 + i])
        for i, source in enumerate((fact_weight_hbm, dim_weight_hbm))
    ]
    pieces = []
    for first, source in ((0, dim_hbm), (dim_hbm.shape[0], fact_hbm)):
        for start in range(0, source.shape[0], PIECE):
            pieces.append(
                pltpu.make_async_copy(
                    source.at[pl.ds(start, PIECE)],
                    table.at[pl.ds(first + start, PIECE)],
                    sems.at[len(loads) + len(pieces)],
                )
            )
    for copy in loads + pieces:
        copy.start()
    for load in loads:
        load.wait()
    place_facts(
        side_ref[0],
        given[0:1, :],
        given[1:2, :],
        given[2:3, :],
        place_ref,
        meta_ref,
        rank_hits_ref,
    )
    terms = jnp.concatenate([stacked_row(weights[i : i + 1, :]) for i in range(2)], 0)
    for copy in pieces:
        copy.wait()
    parts = dot_nt(terms, table[...])
    for start, rows in ((8, range(DIM_ROWS)), (0, range(DIM_ROWS, SCORE_ROWS))):
        part = jnp.sum(
            parts[start : start + 8, rows[0] * LANES : (rows[-1] + 1) * LANES], 0, keepdims=True
        )
        for i, row in enumerate(rows):
            out_ref[0, row : row + 1, :] = part[:, i * LANES : (i + 1) * LANES]
    for peer in range(1, PEERS):
        out_ref[peer] = out_ref[0]


def places(place_ref):
    place = place_ref[...]
    return place & (OWNERS - 1), place >> LABEL_BIT


def pack_kernel(
    recv_ref, place_ref, meta_ref, rank_hits_ref, out_ref, dims_ref, facts_ref, left_ref
):
    total = recv_ref[0]
    for peer in range(1, PEERS):
        total = total + recv_ref[peer]
    dims_ref[...] = total[:DIM_ROWS]
    owner, _ = places(place_ref)
    for i in range(FACT_ROWS):
        cut = slice(i * LANES, (i + 1) * LANES)
        mine = hits(owner[:, cut], OWNERS)
        for part, value in enumerate(split3(total[DIM_ROWS + i : DIM_ROWS + i + 1])):
            left_ref[part * OWNERS : (part + 1) * OWNERS, cut] = jnp.where(mine, value, 0.0).astype(bf16)
    packed = dot_nt(left_ref[...], rank_hits_ref[...])
    packed = packed[:OWNERS] + packed[OWNERS : 2 * OWNERS] + packed[2 * OWNERS :]
    facts_ref[...] = packed
    for chip in range(CHIPS):
        out_ref[chip, :DIM_ROWS, :] = total[:DIM_ROWS]
        for other in range(2):
            row, slot = DIM_ROWS + other, other * CHIPS + chip
            out_ref[chip, row : row + 1, :] = packed[slot : slot + 1]
            out_ref[chip, row + 2 : row + 3, :] = meta_ref[slot : slot + 1, :]


def stacked(value, count=3):
    return jnp.concatenate(split3(value)[:count], 0).astype(bf16)


def summed(parts, count):
    total = parts[:count]
    for start in range(count, parts.shape[0], count):
        total = total + parts[start : start + count]
    return total


def taken(value, row):
    return jnp.sum(jnp.where(hits(row, value.shape[0]), value, 0.0), 0, keepdims=True)


def sigmoid(value):
    return 1.0 / (1.0 + jnp.exp(-value))


def half(
    other, recv_ref, dims_ref, facts_ref, meta_ref, place_ref, rank_hits_ref, row_hits_ref, scratch
):
    home_ref, own_ref, code_ref, low_ref, left_ref = scratch
    slots = slice(other * CHIPS, (other + 1) * CHIPS)
    meta = meta_ref[slots, :].astype(jnp.int32)
    dims = stacked(dims_ref[...])
    for chip in range(CHIPS):
        cut = slice(chip * LANES, (chip + 1) * LANES)
        parts = dot_nn(stacked(recv_ref[chip, :DIM_ROWS, :]), row_hits_ref[:, cut])
        home_ref[chip : chip + 1, :] = taken(
            summed(parts, DIM_ROWS), (meta[chip : chip + 1] >> 7) & (DIM_ROWS - 1)
        )
        row = DIM_ROWS + other
        code = recv_ref[chip, row + 2 : row + 3, :].astype(jnp.int32)
        code_ref[:, cut] = code
        low_ref[:, cut] = onehot(code & (LANES - 1), LANES)
        own_ref[:, cut] = recv_ref[chip, row : row + 1, :]
    prob = stacked(sigmoid(home_ref[...] + facts_ref[slots, :]), 2)
    prob = taken(
        summed(dot_nn(prob, rank_hits_ref[...]), CHIPS), places(place_ref)[0] - other * CHIPS
    )
    code = code_ref[...]
    mine = hits((code >> 7) & (DIM_ROWS - 1), DIM_ROWS)
    score = summed(dot_nn(dims, low_ref[...]), DIM_ROWS)
    score = own_ref[...] + jnp.sum(jnp.where(mine, score, 0.0), 0, keepdims=True)
    residual = (sigmoid(score) - ((code >> LABEL_BIT) & 1).astype(f32)) * (
        code >> VALID_BIT
    ).astype(f32)
    for part, value in enumerate(split3(residual)[:2]):
        left_ref[part * DIM_ROWS : (part + 1) * DIM_ROWS, :] = jnp.where(mine, value, 0.0).astype(
            bf16
        )
    return prob, summed(dot_nt(left_ref[...], low_ref[...]), DIM_ROWS)


def same_side_kernel(
    recv_ref,
    dims_ref,
    facts_ref,
    meta_ref,
    place_ref,
    rank_hits_ref,
    prob_ref,
    sums_ref,
    row_hits_ref,
    here_ref,
    *scratch,
):
    meta = meta_ref[...].astype(jnp.int32) & (LANES - 1)
    for chip in range(CHIPS):
        cut = slice(chip * LANES, (chip + 1) * LANES)
        here_ref[:, cut] = onehot(meta[chip : chip + 1], LANES)
    prob_ref[...], sums_ref[...] = half(
        0, recv_ref, dims_ref, facts_ref, meta_ref, place_ref, rank_hits_ref, here_ref, scratch
    )
    for chip in range(CHIPS):
        cut = slice(chip * LANES, (chip + 1) * LANES)
        row_hits_ref[:, cut] = onehot(meta[CHIPS + chip : CHIPS + chip + 1], LANES)


def grads_kernel(
    recv_ref,
    dims_ref,
    facts_ref,
    meta_ref,
    place_ref,
    rank_hits_ref,
    row_hits_ref,
    prob_half_ref,
    sums_half_ref,
    fact_ref,
    dim_ref,
    out_ref,
    prob_ref,
    *scratch,
):
    prob, sums = half(
        1, recv_ref, dims_ref, facts_ref, meta_ref, place_ref, rank_hits_ref, row_hits_ref, scratch
    )
    prob = prob + prob_half_ref[...]
    sums = sums + sums_half_ref[...]
    prob_ref[...] = prob
    residual = prob - places(place_ref)[1].astype(f32)
    grad_fact = jnp.sum(dot_nn(stacked_row(residual), fact_ref[...]), 0, keepdims=True)
    rows = jnp.concatenate([stacked_row(sums[i : i + 1]) for i in range(DIM_ROWS)], 1)
    side = DIM_ROWS // 2 * LANES
    both = dot_nn(
        jnp.concatenate([rows[:, :side], rows[:, side:]], 0),
        jnp.concatenate([dim_ref[:side, :], dim_ref[side:, :]], 1),
    )
    grad_dim = jnp.sum(both[:8, :LANES] + both[8:, LANES:], 0, keepdims=True)
    for owner in range(OWNERS):
        out_ref[owner, 0:1, :] = grad_fact
        out_ref[owner, 1:2, :] = grad_dim


def update_kernel(recv_ref, fact_weight_ref, dim_weight_ref, fact_out_ref, dim_out_ref):
    total = recv_ref[0]
    for peer in range(1, OWNERS):
        total = total + recv_ref[peer]
    scale = 0.5 / (OWNERS * FACTS_HERE) ** 0.5
    fact_out_ref[...] = fact_weight_ref[...] - scale * total[0:1]
    dim_out_ref[...] = dim_weight_ref[...] - scale * total[1:2]


HALF_SCRATCH = [
    pltpu.VMEM((CHIPS, LANES), f32),
    pltpu.VMEM((1, CHIPS * LANES), f32),
    pltpu.VMEM((1, CHIPS * LANES), jnp.int32),
    pltpu.VMEM((LANES, CHIPS * LANES), bf16),
    pltpu.VMEM((2 * DIM_ROWS, CHIPS * LANES), bf16),
]


def call(kernel, outs, scratch=(), in_specs=None, flops=None):
    extra = {} if in_specs is None else {"in_specs": in_specs}
    if flops is not None:
        extra["cost_estimate"] = pl.CostEstimate(
            flops=flops, bytes_accessed=1 << 20, transcendentals=0
        )
    return pl.pallas_call(
        kernel,
        name=kernel.__name__,
        out_shape=outs,
        scratch_shapes=list(scratch),
        compiler_params=pltpu.CompilerParams(vmem_limit_bytes=32 << 20),
        **extra,
    )


def exchange(value, axis, groups=None):
    return lax.all_to_all(
        value, axis, split_axis=0, concat_axis=0, tiled=True, axis_index_groups=groups
    )


def shards(fact_table, dim_table, fact_weight, dim_weight, bucket, row_index, labels):
    bucket = bucket.reshape(1, FACTS_HERE)
    row_index = row_index.reshape(1, FACTS_HERE)
    labels = labels.reshape(1, FACTS_HERE)
    fact_weight = fact_weight.reshape(1, LANES)
    dim_weight = dim_weight.reshape(1, LANES)
    side = side_of(lax.axis_index("rows")).reshape(1)
    partial, place, meta, rank_hits = call(
        prepare_kernel,
        [
            pltpu.VMEM((PEERS, SCORE_ROWS, LANES), f32),
            pltpu.VMEM((1, FACTS_HERE), jnp.int32),
            pltpu.VMEM((OWNERS, LANES), f32),
            pltpu.VMEM((LANES, FACTS_HERE), bf16),
        ],
        [
            pltpu.VMEM((3, FACTS_HERE), jnp.int32),
            pltpu.VMEM((2, LANES), f32),
            pltpu.VMEM((SCORE_ROWS * LANES, LANES), bf16),
            pltpu.SemaphoreType.DMA((5 + (len(fact_table) + len(dim_table)) // PIECE,)),
        ],
        [pl.BlockSpec(memory_space=pltpu.SMEM)]
        + [pl.BlockSpec(memory_space=pltpu.HBM)] * 7,
    )(
        side,
        *[
            pltpu.with_memory_space_constraint(array, pltpu.HBM)
            for array in (
                bucket,
                row_index,
                labels,
                fact_table,
                dim_table,
                fact_weight,
                dim_weight,
            )
        ],
    )
    partial = exchange(partial, "feat", [FEAT_ORDER])
    blocks, dims, facts = call(
        pack_kernel,
        [
            pltpu.VMEM((CHIPS, BLOCK_ROWS, LANES), f32),
            pltpu.VMEM((DIM_ROWS, LANES), f32),
            pltpu.VMEM((OWNERS, LANES), f32),
        ],
        [pltpu.VMEM((3 * OWNERS, FACTS_HERE), bf16)],
    )(partial, place, meta, rank_hits)
    blocks = exchange(
        blocks, "rows", SIDES
    )
    other_blocks = lax.ppermute(blocks, "rows", [(i, i ^ 1) for i in range(OWNERS)])
    prob_half, sums_half, row_hits = call(
        same_side_kernel,
        [
            pltpu.VMEM((1, FACTS_HERE), f32),
            pltpu.VMEM((DIM_ROWS, LANES), f32),
            pltpu.VMEM((LANES, CHIPS * LANES), bf16),
        ],
        [pltpu.VMEM((LANES, CHIPS * LANES), bf16)] + HALF_SCRATCH,
        flops=1 << 31,
    )(blocks, dims, facts, meta, place, rank_hits)
    grads, prob = call(
        grads_kernel,
        [
            pltpu.VMEM((OWNERS, 2, LANES), f32),
            jax.ShapeDtypeStruct((1, FACTS_HERE), f32),
        ],
        HALF_SCRATCH,
    )(
        other_blocks,
        dims,
        facts,
        meta,
        place,
        rank_hits,
        row_hits,
        prob_half,
        sums_half,
        fact_table,
        dim_table,
    )
    grads = exchange(grads, "rows", [ROW_ORDER])
    new_fact, new_dim = call(update_kernel, [jax.ShapeDtypeStruct((1, LANES), f32)] * 2)(
        grads, fact_weight, dim_weight
    )
    return new_fact.reshape(-1), new_dim.reshape(-1), prob.reshape(-1)


def solution(mesh):
    return jax.shard_map(
        shards,
        mesh=mesh,
        in_specs=(
            P("rows", "feat"),
            P("rows", "feat"),
            P("feat"),
            P("feat"),
            P("rows", None),
            P("rows"),
            P("rows"),
        ),
        out_specs=(P("feat"), P("feat"), P("rows")),
        check_vma=False,
    )
```
